256 devices in a mesh: dp: 2 (over core), expert: 8 (over z_hi, x), tensor: 16 (over y, z_lo).
Axes of the slice: x: 4, y: 4, z: 8 (z_hi: 2, z_lo: 4; z = z_hi * 4 + z_lo), core: 2. Of those that a mesh axis runs over, the one named last changes fastest.
Arguments:
- cotangent: bfloat16 [2, 8192, 3072], P('dp', ('expert', 'tensor')), may hold values from -6 to 6
- scales: float32 [2, 8192], P('dp', ('expert', 'tensor')), may hold values from 0.1 to 1
- routes: int32 [2, 8192, 1], P('dp', ('expert', 'tensor')), may hold values from 0 to 7; in each aligned block of 64 rows (0 to 63, 64 to 127, ..., all dimensions but the last counted through in order) at most 16 rows name the same one
- gate: bfloat16 [2, 8, 2048, 8192], P('dp', 'expert', None, 'tensor'), may hold values from -6 to 6
- up: bfloat16 [2, 8, 2048, 8192], P('dp', 'expert', None, 'tensor'), may hold values from -6 to 6
- weight: bfloat16 [8, 8192, 3072], P('expert', 'tensor'), may hold values from -0.0625 to 0.0625
Outputs:
- grad_gate: bfloat16 [2, 8, 2048, 8192], P('dp', 'expert', None, 'tensor')
- grad_up: bfloat16 [2, 8, 2048, 8192], P('dp', 'expert', None, 'tensor')
- weight_grad: bfloat16 [8, 8192, 3072], P('expert', 'tensor', 'dp')
The draws below stay inside these ranges and needn't reach their ends.
Inputs may be any that keep to these rules, and one draw needn't show every extreme that they name: `routes`: in each source device's block of 64 rows at most 16 rows name one expert, and in every draw some block has exactly 16 rows for one expert.
All inputs are finite; a program needn't handle non-finite values.
Results may differ from the reference program's by a relative error of at most 0.0057.
Values may be sent and summed in bfloat16 or wider, within the bound.
No kernel may reach another device: no remote copies, remote signals or barrier semaphores. Data moves between devices by JAX's collectives and lax.ppermute only.
A program may use at most 128 MiB of HBM per device.

```python
import math
import jax
import jax.numpy as jnp
import numpy as np
from jax import lax

D = 3072
FF = 8192
TOK_DEV = 64
EXPERTS = 8
REPLICAS = 2
TOKENS_REP = 8192
SLOT = 16
CAPACITY = 2048
N_DP = 2
N_EXPERT = 8
N_TENSOR = 16


def steps_of(own_key, extent, shards, least, high):
    loudness, own = 1.0, jax.random.fold_in(own_key, 6)
    for dim, shards_of in shards:
        heights = jnp.exp(jax.random.uniform(jax.random.fold_in(own, dim), (shards_of,), jnp.float32, least / len(shards), high / len(shards)))
        loudness = loudness * jnp.repeat(heights, extent[dim] // shards_of).reshape([-1 if axis == dim else 1 for axis in range(len(extent))])
    return loudness


def shared_out(rng, own, number, rows, count, top, bound, slope):
    ranking = jax.random.permutation(rng, count)
    heavy_load, ordinary = portions_of(count, rows * top, bound, slope, True), portions_of(count, rows * top, bound, slope, False)
    places = jnp.arange(count)

    def named(lengths, offset_by):
        used = int((lengths > 0).sum())
        fixed = max(1, used // 4)
        passed = fixed + (places - fixed + offset_by * (used - fixed)) % max(1, count - fixed)
        return jnp.zeros((count,), jnp.int32).at[ranking[jnp.where(places < fixed, places, passed)]].set(jnp.asarray(lengths, jnp.int32))

    lengths = jnp.where(number % 4 == 0, named(heavy_load, number // 4), named(ordinary, number - number // 4 - 1))
    mixed = jax.random.permutation(jax.random.fold_in(own, 3), count)
    source_of, receiver = mixed[0:count // 2 * 2:2], mixed[1:count // 2 * 2:2]
    margin = jnp.minimum(lengths[source_of] - 1, bound - lengths[receiver]) // 2
    margin = jnp.where((source_of == ranking[0]) | (receiver == ranking[0]) | (lengths[receiver] == 0), 0, jnp.maximum(margin, 0))
    passed = jax.random.randint(jax.random.fold_in(own, 4), (count // 2,), 0, 1 << 20) % (margin + 1)
    lengths = lengths.at[source_of].add(-passed).at[receiver].add(passed)
    labels = jnp.searchsorted(jnp.cumsum(lengths), jnp.arange(rows * top), side="right").astype(jnp.int32)
    listing = labels.reshape(top, rows).T
    listing = listing[jax.random.permutation(jax.random.fold_in(own, 1), rows)]
    offset_by = jax.random.randint(jax.random.fold_in(own, 2), (rows, 1), 0, top)
    return jnp.take_along_axis(listing, (jnp.arange(top)[None, :] + offset_by) % top, axis=1)


def portions_of(amount, total, bound, lean, full):
    loads = [(1 << 20) // math.isqrt(grade ** lean) + 1 for grade in range(1, amount + 1)]
    largest = bound if full else min(bound, max(-(-total // amount), total * loads[0] // sum(loads)))
    least = 1 if total - largest >= amount - 1 else 0
    given, spare = [largest] + [least] * (amount - 1), total - largest - least * (amount - 1)
    while spare > 0:
        candidates = [i for i in range(1, amount) if given[i] < largest] or [i for i in range(1, amount) if given[i] < bound]
        whole, budget = sum([loads[i] for i in candidates]), spare
        for i in candidates:
            extra = min(bound - given[i], max(1, budget * loads[i] // whole), spare)
            given[i] = given[i] + extra
            spare = spare - extra
    return np.array(given)


def scatter_about(rng, shape, spread, bound, cuts=(), kind=jnp.bfloat16):
    drawn = jax.random.normal(rng, shape, jnp.float32) * spread
    if len(cuts) > 0:
        drawn = steps_of(rng, shape, cuts, -0.22, 0.18) * drawn
    return jnp.clip(drawn, min=-bound, max=bound).astype(kind)


def setup_inputs(seed: int = 0) -> dict:
    key_of = jax.random.split(jax.random.key(seed), 7)
    cotangent = scatter_about(key_of[0], (REPLICAS, TOKENS_REP, D), 1.0, 6.0, ((0, 2), (1, 128)))
    scales = jnp.clip(jnp.exp(math.log(1.0) - 2.3025851 * jax.random.uniform(key_of[1], (REPLICAS, TOKENS_REP), jnp.float32) ** steps_of(key_of[1], (REPLICAS, TOKENS_REP), ((0, 2), (1, 128)), -0.2, 0.2)), 0.1, 1.0)
    routes_keys = jax.random.split(jax.random.fold_in(key_of[2], 1), REPLICAS * TOKENS_REP // TOK_DEV)
    routes_turns = jax.random.permutation(jax.random.fold_in(key_of[2], 3), REPLICAS * TOKENS_REP // TOK_DEV)
    routes = jax.vmap(lambda own, number: shared_out(jax.random.fold_in(key_of[2], 2), own, number, TOK_DEV, EXPERTS, 1, SLOT, 2))(routes_keys, routes_turns).reshape((REPLICAS, TOKENS_REP, 1))
    gate = scatter_about(key_of[3], (REPLICAS, EXPERTS, CAPACITY, FF), 1.0, 6.0, ((0, 2), (1, 8), (3, 16)))
    up = scatter_about(key_of[4], (REPLICAS, EXPERTS, CAPACITY, FF), 1.0, 6.0, ((0, 2), (1, 8), (3, 16)))
    weight = scatter_about(key_of[5], (EXPERTS, FF, D), FF ** -0.5, 0.0625, ((0, 8), (1, 16)))
    return {"cotangent": cotangent, "scales": scales, "routes": routes, "gate": gate, "up": up, "weight": weight}


def reference(cotangent, scales, routes, gate, up, weight):
    grad_gates = []
    grad_ups = []
    total = jnp.zeros((EXPERTS, FF, D), jnp.float32)
    for replica in range(N_DP):
        expert_ids = routes[replica, :, 0]
        onehot = (expert_ids[:, None] == jnp.arange(EXPERTS, dtype=jnp.int32)[None, :]).astype(jnp.int32)
        blocks = onehot.reshape(-1, TOK_DEV, EXPERTS)
        before = (jnp.cumsum(blocks, axis=1) - blocks).reshape(-1, EXPERTS)
        slot_in = lax.optimization_barrier(jnp.sum(before * onehot, axis=1)).astype(jnp.int32)
        source = jnp.arange(TOKENS_REP, dtype=jnp.int32) // TOK_DEV
        slot_row = source % N_TENSOR * (N_EXPERT * SLOT) + source // N_TENSOR * SLOT + slot_in
        scaled = (cotangent[replica].astype(jnp.float32) * scales[replica][:, None]).astype(jnp.bfloat16)
        buffer = jnp.zeros((EXPERTS, CAPACITY, D), jnp.bfloat16).at[expert_ids, slot_row].set(scaled)
        gate_list = []
        up_list = []
        for index in range(EXPERTS):
            rows = buffer[index]
            grad_hidden = jnp.dot(rows, weight[index].T, preferred_element_type=jnp.float32)
            pre_gate = gate[replica, index].astype(jnp.float32)
            up_value = up[replica, index].astype(jnp.float32)
            sig = jax.nn.sigmoid(pre_gate)
            silu = pre_gate * sig
            gate_list.append((grad_hidden * up_value * sig * (1.0 + pre_gate * (1.0 - sig))).astype(jnp.bfloat16))
            up_list.append((grad_hidden * silu).astype(jnp.bfloat16))
            hidden = (silu * up_value).astype(jnp.bfloat16)
            total = total.at[index].add(jnp.dot(hidden.T, rows, preferred_element_type=jnp.float32))
        grad_gates.append(jnp.stack(gate_list))
        grad_ups.append(jnp.stack(up_list))
    factor = 1.0 / jnp.sqrt(jnp.float32(N_DP * TOKENS_REP))
    weight_grad = (total * factor).astype(jnp.bfloat16)
    return (jnp.stack(grad_gates), jnp.stack(grad_ups), weight_grad)
```

```python
import functools

import jax
import jax.numpy as jnp
from jax import lax
from jax.experimental import pallas as pl
from jax.experimental.pallas import tpu as pltpu
from jax.sharding import PartitionSpec as P

AX = ("dp", "expert", "tensor")
NX, NY, NZ = 4, 4, 4
SLOT = 16
HALF = NX * SLOT
ANY = pl.ANY
VMEM_LIMIT = 48 * 1024 * 1024


def chip_perm(fn):
    pairs = []
    for c in range(2):
        for z in range(2 * NZ):
            for x in range(NX):
                for y in range(NY):
                    to = fn(c, x, y, z)
                    if to is not None:
                        pairs.append((flat(c, x, y, z), flat(*to)))
    return pairs


def flat(c, x, y, z):
    x, y, z = x % NX, y % NY, z % (2 * NZ)
    return (c * 2 * NX + (z // NZ) * NX + x) * NY * NZ + y * NZ + z % NZ


X_STEP = [chip_perm(lambda c, x, y, z, k=k: (c, x + k, y, z)) for k in range(NX)]
Y_STEP = chip_perm(lambda c, x, y, z: (c, x, y + 1 - 2 * c, z))
Z_MIRROR = chip_perm(lambda c, x, y, z: (c, x, y, 2 * NZ - 1 - z))
Z_PAIR = chip_perm(lambda c, x, y, z: (c, x, y, z ^ 1))
Z_MIDDLE = chip_perm(lambda c, x, y, z: (c, x, y, z ^ 3) if z % NZ in (1, 2) else None)
Z_OUT = chip_perm(lambda c, x, y, z: (c, x, y, z ^ 1) if z % NZ in (1, 2) else None)
DP_SWAP = chip_perm(lambda c, x, y, z: (1 - c, x, y, z))


def send(a, pairs):
    return lax.ppermute(a, AX, pairs)


def dispatch_kernel(place, cot, scales, ids_col, ids_row, u0, u1, u2, u3, v):
    tok = cot.shape[0]
    x, zhi = place[0], place[1]
    col, row = ids_col[...], ids_row[...]
    shape = (tok, tok)
    earlier = lax.broadcasted_iota(jnp.int32, shape, 0) < lax.broadcasted_iota(jnp.int32, shape, 1)
    same = jnp.where((col == row) & earlier, 1.0, 0.0)
    slot = jnp.sum(same, axis=0, keepdims=True).astype(jnp.int32)
    other = jnp.where((row >> 2) == zhi, 0, HALF)
    target = other + ((row - x) & (NX - 1)) * SLOT + slot
    pick = lax.broadcasted_iota(jnp.int32, (2 * HALF, tok), 0) == target
    pick = jnp.where(pick, 1.0, 0.0).astype(jnp.bfloat16)
    scaled = (cot[...].astype(jnp.float32) * scales[...]).astype(jnp.bfloat16)
    out = jnp.dot(pick, scaled, preferred_element_type=jnp.float32).astype(jnp.bfloat16)
    for k, ref in enumerate((u0, u1, u2, u3)):
        ref[...] = out[k * SLOT:(k + 1) * SLOT]
    v[...] = out[HALF:]


def dispatch(place, cot, scales, ids):
    tok, width = cot.shape
    block = jax.ShapeDtypeStruct((SLOT, width), jnp.bfloat16)
    vmem = pl.BlockSpec(memory_space=pltpu.VMEM)
    return pl.pallas_call(
        dispatch_kernel,
        out_shape=(block,) * NX + (jax.ShapeDtypeStruct((HALF, width), jnp.bfloat16),),
        in_specs=[pl.BlockSpec(memory_space=pltpu.SMEM)] + [vmem] * 4,
        out_specs=(vmem,) * (NX + 1),
        name="dispatch",
    )(place, cot, scales.reshape(tok, 1), ids.reshape(tok, 1), ids.reshape(1, tok))


def assemble_kernel(place, b0, b1, b2, b3, out):
    x = place[0]
    for k, ref in enumerate((b0, b1, b2, b3)):
        at = pl.multiple_of(((x - k) & (NX - 1)) * SLOT, SLOT)
        out[pl.ds(at, SLOT), :] = ref[...]


def assemble(place, blocks):
    vmem = pl.BlockSpec(memory_space=pltpu.VMEM)
    return pl.pallas_call(
        assemble_kernel,
        out_shape=jax.ShapeDtypeStruct((HALF, blocks[0].shape[1]), jnp.bfloat16),
        in_specs=[pl.BlockSpec(memory_space=pltpu.SMEM)] + [vmem] * NX,
        out_specs=vmem,
        name="assemble",
    )(place, *blocks)


def hidden_grad_kernel(counts, fresh, *refs):
    n = len(counts)
    offs, rows, (wt, gate, up) = refs[0], refs[1:1 + n], refs[1 + n:4 + n]
    rest = refs[4 + n:] if fresh else refs[6 + n:]
    gg, gu, rows_s, wt_s, gate_s, up_s, gg_s, gu_s, sems, row_sems, blk_sems, out_sems = rest
    total = sum(counts)
    blocks = total // HALF
    w_copy = pltpu.make_async_copy(wt, wt_s, sems.at[0])
    w_copy.start()
    row_copies, at = [], 0
    for i, m in enumerate(counts):
        row_copies.append(pltpu.make_async_copy(rows[i], rows_s.at[pl.ds(at, m)], row_sems.at[i]))
        row_copies[-1].start()
        at += m
    blk_copies, out_copies = [], []
    for b in range(blocks):
        here = pl.ds(b * HALF, HALF)
        there = pl.ds(pl.multiple_of(offs[b], HALF), HALF)
        for k, (src, dst) in enumerate(((gate, gate_s), (up, up_s))):
            blk_copies.append(pltpu.make_async_copy(src.at[there], dst.at[here], blk_sems.at[k, b]))
            blk_copies[-1].start()
        for k, (src, dst) in enumerate(((gg_s, gg), (gu_s, gu))):
            out_copies.append(pltpu.make_async_copy(src.at[here], dst.at[there], out_sems.at[k, b]))
    w_copy.wait()
    for c in row_copies + blk_copies:
        c.wait()
    step = 256 if total % 256 == 0 else 128
    for t in range(total // step):
        here = pl.ds(t * step, step)
        grad = jnp.dot(rows_s[here, :], wt_s[...], preferred_element_type=jnp.float32)
        g = gate_s[here, :].astype(jnp.float32)
        u = up_s[here, :].astype(jnp.float32)
        sig = jax.nn.sigmoid(g)
        gg_s[here, :] = (grad * u * sig * (1.0 + g * (1.0 - sig))).astype(jnp.bfloat16)
        gu_s[here, :] = (grad * (g * sig)).astype(jnp.bfloat16)
        per = step // HALF
        for c in out_copies[2 * per * t:2 * per * (t + 1)]:
            c.start()
    for c in out_copies:
        c.wait()


def hidden_grads(rows, offs, wt, gate, up, outs):
    counts = tuple(r.shape[0] for r in rows)
    total, blocks = sum(counts), sum(counts) // HALF
    width, units = wt.shape
    fresh = outs is None
    n = len(rows)
    out = jax.ShapeDtypeStruct(gate.shape, jnp.bfloat16)
    args = (offs, *rows, wt, gate, up) + (() if fresh else tuple(outs))
    tile = pltpu.VMEM((total, units), jnp.bfloat16)
    return pl.pallas_call(
        functools.partial(hidden_grad_kernel, counts, fresh),
        out_shape=(out, out),
        in_specs=[pl.BlockSpec(memory_space=pltpu.SMEM)] + [pl.BlockSpec(memory_space=ANY)] * (len(args) - 1),
        out_specs=(pl.BlockSpec(memory_space=ANY),) * 2,
        scratch_shapes=[
            pltpu.VMEM((total, width), jnp.bfloat16),
            pltpu.VMEM((width, units), jnp.bfloat16),
            tile, tile, tile, tile,
            pltpu.SemaphoreType.DMA((1,)),
            pltpu.SemaphoreType.DMA((n,)),
            pltpu.SemaphoreType.DMA((2, blocks)),
            pltpu.SemaphoreType.DMA((2, blocks)),
        ],
        input_output_aliases={} if fresh else {n + 4: 0, n + 5: 1},
        compiler_params=pltpu.CompilerParams(vmem_limit_bytes=VMEM_LIMIT),
        cost_estimate=pl.CostEstimate(
            flops=2 * total * width * units,
            bytes_accessed=2 * (total * width + width * units + 4 * total * units),
            transcendentals=total * units,
        ),
        name="hidden_grads",
    )(*args)


def weight_grad_kernel(counts, fresh, *refs):
    n = len(counts)
    half, offs, rows, hid = refs[0], refs[1], refs[2:2 + n], refs[2 + n]
    rest = refs[3 + n:]
    acc = None if fresh else rest[0]
    out, hid_s, hid_t, rows_s, sems = rest[0 if fresh else 1:]
    blocks = sum(counts) // HALF

    @pl.when(pl.program_id(0) == 0)
    def _():
        copies = []
        for b in range(blocks):
            there = pl.ds(pl.multiple_of(offs[b], HALF), HALF)
            copies.append(pltpu.make_async_copy(hid.at[there], hid_s.at[pl.ds(b * HALF, HALF)], sems.at[b]))
            copies[-1].start()
        for c in copies:
            c.wait()
        hid_t[...] = hid_s[...].T

    at = 0
    for i, m in enumerate(counts):
        rows_s[pl.ds(at, m), :] = rows[i][...]
        at += m
    part = jnp.dot(hid_t[...], rows_s[...], preferred_element_type=jnp.float32)
    out[...] = part if fresh else acc[...] + part


def weight_grad_part(rows, half, offs, hid, acc):
    counts = tuple(r.shape[0] for r in rows)
    total, width, units = sum(counts), rows[0].shape[1], hid.shape[1]
    cols = 512
    steps = width // 2 // cols
    fresh = acc is None
    n = len(rows)
    acc_spec = pl.BlockSpec((units, cols), lambda j, h, o: (0, j))
    grid_spec = pltpu.PrefetchScalarGridSpec(
        num_scalar_prefetch=2,
        grid=(steps,),
        in_specs=[pl.BlockSpec((m, cols), lambda j, h, o: (0, h[0] * steps + j)) for m in counts]
        + [pl.BlockSpec(memory_space=ANY)] + ([] if fresh else [acc_spec]),
        out_specs=acc_spec,
        scratch_shapes=[
            pltpu.VMEM((total, units), jnp.bfloat16),
            pltpu.VMEM((units, total), jnp.bfloat16),
            pltpu.VMEM((total, cols), jnp.bfloat16),
            pltpu.SemaphoreType.DMA((total // HALF,)),
        ],
    )
    args = (half, offs, *rows, hid) + (() if fresh else (acc,))
    return pl.pallas_call(
        functools.partial(weight_grad_kernel, counts, fresh),
        out_shape=jax.ShapeDtypeStruct((units, width // 2), jnp.float32),
        grid_spec=grid_spec,
        input_output_aliases={} if fresh else {n + 3: 0},
        compiler_params=pltpu.CompilerParams(vmem_limit_bytes=VMEM_LIMIT),
        cost_estimate=pl.CostEstimate(
            flops=total * width * units,
            bytes_accessed=total * width + 2 * total * units + 4 * units * width,
            transcendentals=0,
        ),
        name="weight_grad_part",
    )(*args)


def gather_z(own, inner):
    near = send(own, Z_PAIR)
    mid1 = send(own, Z_MIDDLE)
    mid2 = send(near, Z_MIDDLE)
    out1 = send(mid1, Z_OUT)
    out2 = send(mid2, Z_OUT)
    far = jnp.concatenate([jnp.where(inner, mid1, out1), jnp.where(inner, mid2, out2)], axis=0)
    return near, far


def ring_y(own):
    parts = [own]
    for _ in range(NY - 1):
        parts.append(send(parts[-1], Y_STEP))
    return parts


def per_device(cotangent, scales, routes, gate, up, weight):
    dp = lax.axis_index("dp")
    expert = lax.axis_index("expert")
    tensor = lax.axis_index("tensor")
    x, zhi = expert % NX, expert // NX
    y, z = tensor // NZ, tensor % NZ
    gate, up, weight = gate[0, 0], up[0, 0], weight[0]
    inner = (z == 1) | (z == 2)

    place = jnp.stack([x, zhi]).astype(jnp.int32)
    *u_blocks, v_send = dispatch(place, cotangent[0], scales[0], routes[0, :, 0])
    v_here = send(v_send, Z_MIRROR)
    u_own = assemble(place, [u_blocks[0]] + [send(u_blocks[k], X_STEP[k]) for k in range(1, NX)])
    v_blocks = [v_here[k * SLOT:(k + 1) * SLOT] for k in range(NX)]
    v_own = assemble(place, [v_blocks[0]] + [send(v_blocks[k], X_STEP[k]) for k in range(1, NX)])

    u_near, u_far = gather_z(u_own, inner)
    v_near, v_far = gather_z(v_own, inner)

    far1 = jnp.where(z < 2, 2, 1)
    far2 = jnp.where(z < 2, 3, 0)
    items = [
        (u_own, 0, [z]),
        (u_near, 0, [z ^ 1]),
        (u_far, 0, [far1, far2]),
        (jnp.concatenate([v_own, v_near], axis=0), 1, [z, z ^ 1]),
        (v_far, 1, [far1, far2]),
    ]

    def offsets(kind, zs):
        at = []
        for k in range(NY):
            yy = (y - k * (1 - 2 * dp)) % NY
            for zz in zs:
                src, hi = (zz, zhi) if kind == 0 else (NZ - 1 - zz, 1 - zhi)
                at.append((yy * NZ + src) * (2 * HALF) + hi * HALF)
        return jnp.stack(at).astype(jnp.int32)

    wt = weight.T
    gate_f = gate.astype(jnp.float32)
    hid = (gate_f * jax.nn.sigmoid(gate_f) * up.astype(jnp.float32)).astype(jnp.bfloat16)
    theirs = (1 - dp).astype(jnp.int32).reshape(1)
    mine = dp.astype(jnp.int32).reshape(1)

    gathered = [(ring_y(own), offsets(kind, zs)) for own, kind, zs in items]
    outs = None
    for rows, offs in gathered:
        outs = hidden_grads(rows, offs, wt, gate, up, outs)
    groups = [gathered[0:3], gathered[3:4], gathered[4:5]]
    sums = [None, None]
    for group in groups:
        rows = [r for part in group for r in part[0]]
        offs = jnp.concatenate([part[1] for part in group])
        sums = [weight_grad_part(rows, h, offs, hid, s) for h, s in zip((theirs, mine), sums)]
    got = send(sums[0], DP_SWAP)
    n_tok = 2 * 64 * 8 * 16
    factor = 1.0 / jnp.sqrt(jnp.float32(n_tok))
    weight_grad = ((sums[1] + got) * factor).astype(jnp.bfloat16)
    return (outs[0][None, None], outs[1][None, None], weight_grad[None])


def solution(mesh):
    in_specs = (
        P("dp", ("expert", "tensor"), None),
        P("dp", ("expert", "tensor")),
        P("dp", ("expert", "tensor"), None),
        P("dp", "expert", None, "tensor"),
        P("dp", "expert", None, "tensor"),
        P("expert", "tensor", None),
    )
    out_specs = (
        P("dp", "expert", None, "tensor"),
        P("dp", "expert", None, "tensor"),
        P("expert", "tensor", "dp"),
    )
    return jax.shard_map(
        per_device, mesh=mesh, in_specs=in_specs, out_specs=out_specs, check_vma=False
    )
```

```python
import functools

import jax
import jax.numpy as jnp
from jax import lax
from jax.experimental import pallas as pl
from jax.experimental.pallas import tpu as pltpu
from jax.sharding import PartitionSpec as P

AX = ("dp", "expert", "tensor")
NX, NY, NZ = 4, 4, 4
SLOT = 16
HALF = NX * SLOT
ANY = pl.ANY
VMEM_LIMIT = 62 * 1024 * 1024
PARAMS = pltpu.CompilerParams(vmem_limit_bytes=VMEM_LIMIT)


def chip_perm(fn):
    pairs = []
    for c in range(2):
        for z in range(2 * NZ):
            for x in range(NX):
                for y in range(NY):
                    to = fn(c, x, y, z)
                    if to is not None:
                        pairs.append((flat(c, x, y, z), flat(*to)))
    return pairs


def flat(c, x, y, z):
    x, y, z = x % NX, y % NY, z % (2 * NZ)
    return (c * 2 * NX + (z // NZ) * NX + x) * NY * NZ + y * NZ + z % NZ


X_STEP = [chip_perm(lambda c, x, y, z, k=k: (c, x + k, y, z)) for k in range(NX)]
Y_ON = chip_perm(lambda c, x, y, z: (c, x, y + 1 - 2 * c, z))
Y_BACK = chip_perm(lambda c, x, y, z: (c, x, y - 1 + 2 * c, z))
Z_MIRROR = chip_perm(lambda c, x, y, z: (c, x, y, 2 * NZ - 1 - z))
Z_PAIR = chip_perm(lambda c, x, y, z: (c, x, y, z ^ 1))
Z_MIDDLE = chip_perm(lambda c, x, y, z: (c, x, y, z ^ 3) if z % NZ in (1, 2) else None)
DP_SWAP = chip_perm(lambda c, x, y, z: (1 - c, x, y, z))


def send(a, pairs):
    return lax.ppermute(a, AX, pairs)


def dispatch_kernel(place, cot, scales, ids, *outs):
    tok = cot.shape[0]
    x, zhi = place[0], place[1]
    above = lax.broadcasted_iota(jnp.int32, (tok, tok), 0)
    along = lax.broadcasted_iota(jnp.int32, (tok, tok), 1)
    row = jnp.broadcast_to(ids[...], (tok, tok))
    eye = above == along
    col = jnp.sum(jnp.where(eye, row, 0).astype(jnp.float32), axis=1, keepdims=True)
    col = jnp.broadcast_to(col, (tok, tok)).astype(jnp.int32)
    same = jnp.where((col == row) & (above < along), 1.0, 0.0)
    slot = jnp.sum(same, axis=0, keepdims=True).astype(jnp.int32)
    row = ids[...]
    other = jnp.where((row >> 2) == zhi, 0, SLOT)
    target = ((row - x) & (NX - 1)) * (2 * SLOT) + other + slot
    pick = lax.broadcasted_iota(jnp.int32, (2 * HALF, tok), 0) == target
    pick = jnp.where(pick, 1.0, 0.0).astype(jnp.bfloat16)
    scale = jnp.sum(jnp.where(eye, jnp.broadcast_to(scales[...], (tok, tok)), 0.0), axis=1, keepdims=True)
    scaled = (cot[...].astype(jnp.float32) * scale).astype(jnp.bfloat16)
    out = jnp.dot(pick, scaled, preferred_element_type=jnp.float32).astype(jnp.bfloat16)
    for k, ref in enumerate(outs):
        ref[...] = out[k * 2 * SLOT:(k + 1) * 2 * SLOT]


def dispatch(place, cot, scales, ids):
    tok, width = cot.shape
    block = jax.ShapeDtypeStruct((2 * SLOT, width), jnp.bfloat16)
    vmem = pl.BlockSpec(memory_space=pltpu.VMEM)
    return pl.pallas_call(
        dispatch_kernel,
        out_shape=(block,) * NX,
        in_specs=[pl.BlockSpec(memory_space=pltpu.SMEM)] + [vmem] * 3,
        out_specs=(vmem,) * NX,
        compiler_params=PARAMS,
        name="dispatch",
    )(place, cot, scales, ids.reshape(1, tok))


def assemble_kernel(place, b0, b1, b2, b3, mark, u, v):
    del mark
    x = place[0]
    for k, ref in enumerate((b0, b1, b2, b3)):
        at = pl.multiple_of(((x - k) & (NX - 1)) * SLOT, SLOT)
        u[pl.ds(at, SLOT), :] = ref[:SLOT]
        v[pl.ds(at, SLOT), :] = ref[SLOT:]


def assemble(place, blocks, mark):
    vmem = pl.BlockSpec(memory_space=pltpu.VMEM)
    return pl.pallas_call(
        assemble_kernel,
        out_shape=(jax.ShapeDtypeStruct((HALF, blocks[0].shape[1]), jnp.bfloat16),) * 2,
        in_specs=[pl.BlockSpec(memory_space=pltpu.SMEM)] + [vmem] * NX + [pl.BlockSpec(memory_space=ANY)],
        out_specs=(vmem,) * 2,
        compiler_params=PARAMS,
        name="assemble",
    )(place, *blocks, mark)


def starts_of(sizes):
    at = [0]
    for m in sizes:
        at.append(at[-1] + m)
    return at


COLS = 512


def stage_kernel(counts, sizes, hidden, sums, span, factor, waits, outs, acc, got, *refs):
    n = len(counts)
    refs = list(refs[waits:])

    def take(k, there=True):
        return [refs.pop(0) for _ in range(k)] if there else [None] * k

    first, offs = take(2)
    rows = take(n)
    gate, up = take(2)
    (wt,) = take(1, hidden)
    take(2, outs)
    (acc_in,) = take(1, acc)
    (got_in,) = take(1, got)
    gg, gu = take(2, hidden)
    (sum_out,) = take(1, sums)
    done, rows_s, gate_s, up_s, row_sems, blk_sems = take(6)
    wt_s, gg_s, gu_s, out_sems, w_sem = take(5, hidden)
    hid_t, sum_s, sum_sems = take(3, sums)
    (acc_s,) = take(1, acc)
    (got_s,) = take(1, got)
    total = sum(counts)
    col0 = first[0] * COLS

    blk_copies, out_copies = [], []
    for b, (at, m) in enumerate(zip(starts_of(sizes), sizes)):
        here = pl.ds(at, m)
        there = pl.ds(pl.multiple_of(offs[b], SLOT), m)
        for k, (src, dst) in enumerate(((gate, gate_s), (up, up_s))):
            blk_copies.append((at, pltpu.make_async_copy(src.at[there], dst.at[here], blk_sems.at[k, b])))
            blk_copies[-1][1].start()
        if hidden:
            for k, (src, dst) in enumerate(((gg_s, gg), (gu_s, gu))):
                out_copies.append((at, pltpu.make_async_copy(src.at[here], dst.at[there], out_sems.at[k, b])))
    if hidden:
        w_copy = pltpu.make_async_copy(wt, wt_s, w_sem.at[0])
        w_copy.start()
    row_copies = []
    for i, (at, m) in enumerate(zip(starts_of(counts), counts)):
        src = rows[i]
        if not hidden:
            src = src.at[:, pl.ds(pl.multiple_of(col0, COLS), span * COLS)]
        row_copies.append((at, pltpu.make_async_copy(src, rows_s.at[pl.ds(at, m)], row_sems.at[i])))
        row_copies[-1][1].start()
    acc_copies, got_copies = [], []
    for j in range(span):
        if acc:
            there = pl.ds(pl.multiple_of(col0 + j * COLS, COLS), COLS)
            acc_copies.append(pltpu.make_async_copy(acc_in.at[:, there], acc_s.at[j], sum_sems.at[0, j]))
            acc_copies[-1].start()
        if got:
            there = pl.ds(j * COLS, COLS)
            got_copies.append(pltpu.make_async_copy(got_in.at[:, there], got_s.at[j], sum_sems.at[2, j]))
            got_copies[-1].start()

    def arrived(copies, end):
        for at, c in copies:
            if at < end:
                c.wait()
        return [(at, c) for at, c in copies if at >= end]

    for begin in range(0, total, 256):
        end = min(begin + 256, total)
        here = pl.ds(begin, end - begin)
        blk_copies = arrived(blk_copies, end)
        g = gate_s[here, :].astype(jnp.float32)
        u = up_s[here, :].astype(jnp.float32)
        sig = jax.nn.sigmoid(g)
        silu = g * sig
        if sums:
            hid_t[:, here] = (silu * u).astype(jnp.bfloat16).T
        if hidden and begin == 0:
            w_copy.wait()
        row_copies = arrived(row_copies, end)
        if hidden:
            grad = jnp.dot(rows_s[here, :], wt_s[...], preferred_element_type=jnp.float32)
            gg_s[here, :] = (grad * u * sig * (1.0 + g * (1.0 - sig))).astype(jnp.bfloat16)
            gu_s[here, :] = (grad * silu).astype(jnp.bfloat16)
            for at, c in out_copies:
                if begin <= at < end:
                    c.start()
    sum_copies = []
    for j in range(span if sums else 0):
        part = jnp.dot(hid_t[...], rows_s[:, pl.ds(j * COLS, COLS)], preferred_element_type=jnp.float32)
        if acc:
            acc_copies[j].wait()
            part = acc_s[j] + part
        if got:
            got_copies[j].wait()
            part = part + got_s[j].astype(jnp.float32)
        if factor:
            part = part * factor
        sum_s[j] = part.astype(sum_s.dtype)
        sum_copies.append(
            pltpu.make_async_copy(sum_s.at[j], sum_out.at[:, pl.ds(j * COLS, COLS)], sum_sems.at[1, j])
        )
        sum_copies[-1].start()
    done[0] = 0
    for c in sum_copies + [c for _, c in out_copies]:
        c.wait()


def stage(parts, gate, up, wt=None, outs=None, sums=None, acc=None, got=None, first=None, factor=None, marks=()):
    rows = [p[0] for p in parts]
    sizes = tuple(m for p in parts for m, _ in p[1])
    offs = jnp.stack([at for p in parts for _, at in p[1]]).astype(jnp.int32)
    counts = tuple(r.shape[0] for r in rows)
    total, width, units = sum(counts), rows[0].shape[1], gate.shape[1]
    span = width // COLS // (1 if first is None else 2)
    first = jnp.zeros((1,), jnp.int32) if first is None else first
    hidden = wt is not None
    n, waits = len(rows), len(marks)
    smem, any_ = pl.BlockSpec(memory_space=pltpu.SMEM), pl.BlockSpec(memory_space=ANY)
    args = [*marks, first, offs, *rows, gate, up]
    out_shape = [jax.ShapeDtypeStruct((1,), jnp.int32)]
    out_specs = [smem]
    scratch = [
        pltpu.VMEM((total, width if hidden else span * COLS), jnp.bfloat16),
        pltpu.VMEM((total, units), jnp.bfloat16),
        pltpu.VMEM((total, units), jnp.bfloat16),
        pltpu.SemaphoreType.DMA((n,)),
        pltpu.SemaphoreType.DMA((2, len(sizes))),
    ]
    if sums is not None:
        out_shape = [jax.ShapeDtypeStruct((units, span * COLS), sums)] + out_shape
        out_specs = [any_] + out_specs
    aliases = {}
    if hidden:
        args.append(wt)
        out_shape = [jax.ShapeDtypeStruct(gate.shape, jnp.bfloat16)] * 2 + out_shape
        out_specs = [any_] * 2 + out_specs
        if outs is not None:
            aliases = {len(args): 0, len(args) + 1: 1}
            args += list(outs)
        scratch += [
            pltpu.VMEM((width, units), jnp.bfloat16),
            pltpu.VMEM((total, units), jnp.bfloat16),
            pltpu.VMEM((total, units), jnp.bfloat16),
            pltpu.SemaphoreType.DMA((2, len(sizes))),
            pltpu.SemaphoreType.DMA((1,)),
        ]
    if sums is not None:
        scratch += [
            pltpu.VMEM((units, total), jnp.bfloat16),
            pltpu.VMEM((span, units, COLS), sums),
            pltpu.SemaphoreType.DMA((3, span)),
        ]
    for a in (acc, got):
        if a is not None:
            args.append(a)
            scratch.append(pltpu.VMEM((span, units, COLS), a.dtype))
    moved = sum(a.size * a.dtype.itemsize for a in args[waits + 2:waits + 2 + n]) + 8 * total * units
    moved += 2 * width * units if hidden else 0
    moved += 4 * units * span * COLS if sums is not None else 0
    results = pl.pallas_call(
        functools.partial(
            stage_kernel, counts, sizes, hidden, sums is not None, span, factor, waits,
            outs is not None, acc is not None, got is not None,
        ),
        out_shape=tuple(out_shape),
        in_specs=[smem] * (waits + 2) + [any_] * (len(args) - waits - 2),
        out_specs=tuple(out_specs),
        scratch_shapes=scratch,
        input_output_aliases=aliases,
        compiler_params=PARAMS,
        cost_estimate=pl.CostEstimate(
            flops=2 * total * units * width * (int(hidden) + int(sums is not None)),
            bytes_accessed=moved,
            transcendentals=total * units,
        ),
        name="stage",
    )(*args)
    return results


def after_kernel(*refs):
    del refs


def after(arrays, *marks):
    n = len(arrays)
    return list(pl.pallas_call(
        after_kernel,
        out_shape=tuple(jax.ShapeDtypeStruct(a.shape, a.dtype) for a in arrays),
        in_specs=[pl.BlockSpec(memory_space=pltpu.HBM)] * (n + len(marks)),
        out_specs=(pl.BlockSpec(memory_space=pltpu.HBM),) * n,
        input_output_aliases={i: i for i in range(n)},
        compiler_params=PARAMS,
        cost_estimate=pl.CostEstimate(flops=0, bytes_accessed=0, transcendentals=0),
        name="after",
    )(*arrays, *marks))


def pack_kernel(plan, n, inner, *refs):
    ins, outs, sems = refs[:n], refs[-1 - len(plan):-1], refs[-1]

    def copy(pick):
        copies = []
        for ref, blocks in zip(outs, plan):
            for i, block in enumerate(blocks):
                src, at = block[min(pick, len(block) - 1)]
                src = ins[src].at[pl.ds(at * HALF, HALF)]
                copies.append(pltpu.make_async_copy(src, ref.at[pl.ds(i * HALF, HALF)], sems.at[len(copies)]))
                copies[-1].start()
        for c in copies:
            c.wait()

    @pl.when(inner[0] == 1)
    def _():
        copy(0)

    @pl.when(inner[0] == 0)
    def _():
        copy(1)


def pack(inner, arrays, plan, marks=()):
    width = arrays[0].shape[1]
    return pl.pallas_call(
        functools.partial(pack_kernel, plan, len(arrays)),
        out_shape=tuple(jax.ShapeDtypeStruct((len(b) * HALF, width), jnp.bfloat16) for b in plan),
        in_specs=[pl.BlockSpec(memory_space=pltpu.SMEM)]
        + [pl.BlockSpec(memory_space=ANY)] * (len(arrays) + len(marks)),
        out_specs=(pl.BlockSpec(memory_space=pltpu.VMEM),) * len(plan),
        scratch_shapes=[pltpu.SemaphoreType.DMA((sum(len(b) for b in plan),))],
        compiler_params=PARAMS,
        cost_estimate=pl.CostEstimate(flops=0, bytes_accessed=8 * HALF * width, transcendentals=0),
        name="pack",
    )(inner, *arrays, *marks)


def per_device(cotangent, scales, routes, gate, up, weight):
    dp = lax.axis_index("dp")
    expert = lax.axis_index("expert")
    tensor = lax.axis_index("tensor")
    x, zhi = expert & 3, expert >> 2
    y, z = tensor >> 2, tensor & 3
    gate, up, weight = gate[0, 0], up[0, 0], weight[0]
    inner = ((z == 1) | (z == 2)).astype(jnp.int32).reshape(1)

    wt = weight.T
    place = jnp.stack([x, zhi]).astype(jnp.int32)
    blocks = list(dispatch(place, cotangent[0], scales, routes))
    u_own, v_send = assemble(place, blocks[:1] + [send(blocks[k], X_STEP[k]) for k in range(1, NX)], wt)

    far1 = jnp.where(z < 2, 2, 1)
    far2 = jnp.where(z < 2, 3, 0)

    def blocks_of(items):
        at = []
        for kind, yy, zz in items:
            src, hi = (zz, zhi) if kind == 0 else (NZ - 1 - zz, 1 - zhi)
            at.append((HALF, (yy * NZ + src) * (2 * HALF) + hi * HALF))
        return at

    s = 1 - 2 * dp

    def ring(own, what):
        on = send(own, Y_ON)
        back = send(own, Y_BACK)
        return [
            (a, blocks_of([(kind, yy & 3, zz) for kind, zz in what]))
            for a, yy in ((own, y), (on, y - s), (back, y + s))
        ]

    def pass_on(parts, what, *marks):
        if marks:
            parts[1] = (after([parts[1][0]], *marks)[0], parts[1][1])
        parts.append((send(parts[1][0], Y_ON), blocks_of([(kind, (y - 2 * s) & 3, zz) for kind, zz in what])))

    theirs = ((1 - dp) * 3).astype(jnp.int32).reshape(1)
    mine = (dp * 3).astype(jnp.int32).reshape(1)
    f32 = jnp.float32

    v_own = send(v_send, Z_MIRROR)
    u_near = send(u_own, Z_PAIR)
    u_mid1 = send(u_own, Z_MIDDLE)
    wa = [(0, z)]
    a = ring(u_own, wa)
    pass_on(a, wa)
    b_own, x2 = pack(
        inner, [u_near, v_own, u_mid1],
        ((((0, 0),), ((1, 0),)), (((2, 0),), ((1, 0),))),
        [p[0] for p in a[1:]],
    )
    mid2 = send(b_own, Z_MIDDLE)
    pair2 = send(x2, Z_PAIR)
    wb = [(0, z ^ 1), (1, z)]
    b = ring(b_own, wb)
    *outs, m1 = stage(a, gate, up, wt)
    c_own, v_near = pack(
        inner, [x2, pair2],
        ((((0, 0), (1, 0)), ((1, 1),)), (((1, 1),),)),
        [m1] + [p[0] for p in b[1:]],
    )
    mid3 = send(v_near, Z_MIDDLE)
    pair3 = send(mid2, Z_PAIR)
    pass_on(b, wb)
    wc = [(0, far1), (1, z ^ 1)]
    c = ring(c_own, wc)
    (d_own,) = pack(
        inner, [mid2, pair3],
        ((((0, 0), (1, 0)), ((0, 1), (1, 1))),),
        [p[0] for p in b[3:] + c[1:]],
    )
    pass_on(c, wc)
    wd = [(0, far2), (1, far1)]
    d = ring(d_own, wd)
    pair4 = send(mid3, Z_PAIR)
    *outs, m2 = stage(b, gate, up, wt, outs, marks=(m1,))
    (e_own,) = pack(inner, [mid3, pair4], ((((0, 0), (1, 0)),),), [m2] + [p[0] for p in c[3:]])
    we = [(1, far2)]
    e = ring(e_own, we)
    *outs, m3 = stage(c, gate, up, wt, outs, marks=(m2,))
    pass_on(d, wd, m3)
    acc, m4 = stage(a + b + c, gate, up, sums=f32, marks=(m3,))
    pass_on(e, we, m4)
    *outs, m5 = stage(d[:3] + e[:3], gate, up, wt, outs, marks=(m4,))
    rest = d[:3] + e[:3] + d[3:] + e[3:]
    give, m6 = stage(rest, gate, up, sums=jnp.bfloat16, acc=acc, first=theirs, marks=(m5,))
    got = send(give, DP_SWAP)
    *outs, m7 = stage(rest[6:], gate, up, wt, outs, marks=(m6,))
    n_tok = 2 * 64 * 8 * 16
    factor = 1.0 / n_tok ** 0.5
    weight_grad, _ = stage(
        rest, gate, up, sums=jnp.bfloat16, acc=acc, got=got, first=mine, factor=factor, marks=(m7,)
    )
    return (outs[0][None, None], outs[1][None, None], weight_grad[None])


def solution(mesh):
    in_specs = (
        P("dp", ("expert", "tensor"), None),
        P("dp", ("expert", "tensor")),
        P("dp", ("expert", "tensor"), None),
        P("dp", "expert", None, "tensor"),
        P("dp", "expert", None, "tensor"),
        P("expert", "tensor", None),
    )
    out_specs = (
        P("dp", "expert", None, "tensor"),
        P("dp", "expert", None, "tensor"),
        P("expert", "tensor", "dp"),
    )
    return jax.shard_map(
        per_device, mesh=mesh, in_specs=in_specs, out_specs=out_specs, check_vma=False
    )
```

```python
import functools

import jax
import jax.numpy as jnp
from jax import lax
from jax.experimental import pallas as pl
from jax.experimental.pallas import tpu as pltpu
from jax.sharding import PartitionSpec as P

AX = ("dp", "expert", "tensor")
NX, NY, NZ = 4, 4, 4
SLOT = 16
HALF = NX * SLOT
ANY = pl.ANY
VMEM_LIMIT = 62 * 1024 * 1024
PARAMS = pltpu.CompilerParams(vmem_limit_bytes=VMEM_LIMIT)


def chip_perm(fn):
    pairs = []
    for c in range(2):
        for z in range(2 * NZ):
            for x in range(NX):
                for y in range(NY):
                    to = fn(c, x, y, z)
                    if to is not None:
                        pairs.append((flat(c, x, y, z), flat(*to)))
    return pairs


def flat(c, x, y, z):
    x, y, z = x % NX, y % NY, z % (2 * NZ)
    return (c * 2 * NX + (z // NZ) * NX + x) * NY * NZ + y * NZ + z % NZ


X_STEP = [chip_perm(lambda c, x, y, z, k=k: (c, x + k, y, z)) for k in range(NX)]
Y_ON = chip_perm(lambda c, x, y, z: (c, x, y + 1 - 2 * c, z))
Y_BACK = chip_perm(lambda c, x, y, z: (c, x, y - 1 + 2 * c, z))
Z_MIRROR = chip_perm(lambda c, x, y, z: (c, x, y, 2 * NZ - 1 - z))
Z_PAIR = chip_perm(lambda c, x, y, z: (c, x, y, z ^ 1))
Z_MIDDLE = chip_perm(lambda c, x, y, z: (c, x, y, z ^ 3) if z % NZ in (1, 2) else None)
DP_SWAP = chip_perm(lambda c, x, y, z: (1 - c, x, y, z))


def send(a, pairs):
    return lax.ppermute(a, AX, pairs)


def dispatch_kernel(place, cot, scales, ids, *outs):
    tok = cot.shape[0]
    x, zhi = place[0], place[1]
    above = lax.broadcasted_iota(jnp.int32, (tok, tok), 0)
    along = lax.broadcasted_iota(jnp.int32, (tok, tok), 1)
    row = jnp.broadcast_to(ids[...], (tok, tok))
    eye = above == along
    col = jnp.sum(jnp.where(eye, row, 0).astype(jnp.float32), axis=1, keepdims=True)
    col = jnp.broadcast_to(col, (tok, tok)).astype(jnp.int32)
    same = jnp.where((col == row) & (above < along), 1.0, 0.0)
    slot = jnp.sum(same, axis=0, keepdims=True).astype(jnp.int32)
    row = ids[...]
    other = jnp.where((row >> 2) == zhi, 0, SLOT)
    target = ((row - x) & (NX - 1)) * (2 * SLOT) + other + slot
    pick = lax.broadcasted_iota(jnp.int32, (2 * HALF, tok), 0) == target
    pick = jnp.where(pick, 1.0, 0.0).astype(jnp.bfloat16)
    scale = jnp.sum(jnp.where(eye, jnp.broadcast_to(scales[...], (tok, tok)), 0.0), axis=1, keepdims=True)
    scaled = (cot[...].astype(jnp.float32) * scale).astype(jnp.bfloat16)
    out = jnp.dot(pick, scaled, preferred_element_type=jnp.float32).astype(jnp.bfloat16)
    for k, ref in enumerate(outs):
        ref[...] = out[k * 2 * SLOT:(k + 1) * 2 * SLOT]


def dispatch(place, cot, scales, ids):
    tok, width = cot.shape
    block = jax.ShapeDtypeStruct((2 * SLOT, width), jnp.bfloat16)
    vmem = pl.BlockSpec(memory_space=pltpu.VMEM)
    return pl.pallas_call(
        dispatch_kernel,
        out_shape=(block,) * NX,
        in_specs=[pl.BlockSpec(memory_space=pltpu.SMEM)] + [vmem] * 3,
        out_specs=(vmem,) * NX,
        compiler_params=PARAMS,
        name="dispatch",
    )(place, cot, scales, ids.reshape(1, tok))


def assemble_kernel(place, b0, b1, b2, b3, mark, u, v1, v2, v_s):
    del mark
    x = place[0]
    for k, ref in enumerate((b0, b1, b2, b3)):
        at = pl.multiple_of(((x - k) & (NX - 1)) * SLOT, SLOT)
        u[pl.ds(at, SLOT), :] = ref[:SLOT]
        v_s[pl.ds(at, SLOT), :] = ref[SLOT:]
    v1[...] = v_s[:HALF // 2]
    v2[...] = v_s[HALF // 2:]


def assemble(place, blocks, mark):
    width = blocks[0].shape[1]
    vmem = pl.BlockSpec(memory_space=pltpu.VMEM)
    return pl.pallas_call(
        assemble_kernel,
        out_shape=tuple(jax.ShapeDtypeStruct((m, width), jnp.bfloat16) for m in (HALF, HALF // 2, HALF // 2)),
        in_specs=[pl.BlockSpec(memory_space=pltpu.SMEM)] + [vmem] * NX + [pl.BlockSpec(memory_space=ANY)],
        out_specs=(vmem,) * 3,
        scratch_shapes=[pltpu.VMEM((HALF, width), jnp.bfloat16)],
        compiler_params=PARAMS,
        name="assemble",
    )(place, *blocks, mark)


def starts_of(sizes):
    at = [0]
    for m in sizes:
        at.append(at[-1] + m)
    return at


COLS = 512
SMEM_SPEC = pl.BlockSpec(memory_space=pltpu.SMEM)
ANY_SPEC = pl.BlockSpec(memory_space=ANY)
MARK = jax.ShapeDtypeStruct((1,), jnp.int32)


def hidden_kernel(offs, gate, up, hid_t, done, hid_s):
    blocks = hid_t.shape[1] // HALF
    for b in range(0, blocks, 2):
        for i in range(2):
            there = pl.ds(pl.multiple_of(offs[b + i], HALF), HALF)
            g = gate[there, :].astype(jnp.float32)
            u = up[there, :].astype(jnp.float32)
            hid_s[pl.ds(i * HALF, HALF), :] = (g * jax.nn.sigmoid(g) * u).astype(jnp.bfloat16)
        hid_t[:, pl.ds(b * HALF, 2 * HALF)] = hid_s[...].T
    done[0] = 0


def hidden_rows(offs, gate, up):
    slots, units = gate.shape
    vmem = pl.BlockSpec(memory_space=pltpu.VMEM)
    return pl.pallas_call(
        hidden_kernel,
        out_shape=(jax.ShapeDtypeStruct((units, slots), jnp.bfloat16), MARK),
        in_specs=[SMEM_SPEC, vmem, vmem],
        out_specs=(vmem, SMEM_SPEC),
        scratch_shapes=[pltpu.VMEM((2 * HALF, units), jnp.bfloat16)],
        compiler_params=PARAMS,
        cost_estimate=pl.CostEstimate(
            flops=0, bytes_accessed=6 * slots * units, transcendentals=slots * units
        ),
        name="hidden_rows",
    )(offs, gate, up)


def hidden_grad_kernel(counts, ids, waits, outs, *refs):
    n = len(counts)
    refs = list(refs[waits:])

    def take(k, there=True):
        return [refs.pop(0) for _ in range(k)] if there else [None] * k

    (offs,) = take(1)
    rows = take(n)
    gate, up, wt = take(3)
    take(2, outs)
    gg, gu, done, rows_s, wt_s, gate_s, up_s, gg_s, gu_s, row_sems, in_sems, out_sems, w_sem = take(13)
    total = sum(counts)
    in_copies, out_copies = [], []
    for b in range(total // HALF):
        here = pl.ds(b * HALF, HALF)
        there = pl.ds(pl.multiple_of(offs[ids[b]], HALF), HALF)
        for k, (src, dst) in enumerate(((gate, gate_s), (up, up_s))):
            in_copies.append((b * HALF, pltpu.make_async_copy(src.at[there], dst.at[here], in_sems.at[k, b])))
            in_copies[-1][1].start()
        for k, (src, dst) in enumerate(((gg_s, gg), (gu_s, gu))):
            out_copies.append((b * HALF, pltpu.make_async_copy(src.at[here], dst.at[there], out_sems.at[k, b])))
    w_copy = pltpu.make_async_copy(wt, wt_s, w_sem.at[0])
    w_copy.start()
    for i, (at, m) in enumerate(zip(starts_of(counts), counts)):
        in_copies.append((at, pltpu.make_async_copy(rows[i], rows_s.at[pl.ds(at, m)], row_sems.at[i])))
        in_copies[-1][1].start()
    for begin in range(0, total, 256):
        end = min(begin + 256, total)
        here = pl.ds(begin, end - begin)
        for at, c in in_copies:
            if begin <= at < end:
                c.wait()
        if begin == 0:
            w_copy.wait()
        grad = jnp.dot(rows_s[here, :], wt_s[...], preferred_element_type=jnp.float32)
        g = gate_s[here, :].astype(jnp.float32)
        u = up_s[here, :].astype(jnp.float32)
        sig = jax.nn.sigmoid(g)
        gg_s[here, :] = (grad * u * sig * (1.0 + g * (1.0 - sig))).astype(jnp.bfloat16)
        gu_s[here, :] = (grad * (g * sig)).astype(jnp.bfloat16)
        for at, c in out_copies:
            if begin <= at < end:
                c.start()
    done[0] = 0
    for _, c in out_copies:
        c.wait()


def hidden_grads(parts, offs, gate, up, wt, outs, *marks):
    rows = [p[0] for p in parts]
    ids = tuple(i for p in parts for i in p[1])
    counts = tuple(r.shape[0] for r in rows)
    total, n, waits = sum(counts), len(rows), len(marks)
    width, units = wt.shape
    args = [*marks, offs, *rows, gate, up, wt]
    aliases = {}
    if outs:
        aliases = {len(args): 0, len(args) + 1: 1}
        args += list(outs)
    tile = pltpu.VMEM((total, units), jnp.bfloat16)
    *outs, mark = pl.pallas_call(
        functools.partial(hidden_grad_kernel, counts, ids, waits, bool(outs)),
        out_shape=(jax.ShapeDtypeStruct(gate.shape, jnp.bfloat16),) * 2 + (MARK,),
        in_specs=[SMEM_SPEC] * (waits + 1) + [ANY_SPEC] * (len(args) - waits - 1),
        out_specs=(ANY_SPEC, ANY_SPEC, SMEM_SPEC),
        scratch_shapes=[
            pltpu.VMEM((total, width), jnp.bfloat16),
            pltpu.VMEM((width, units), jnp.bfloat16),
            tile, tile, tile, tile,
            pltpu.SemaphoreType.DMA((n,)),
            pltpu.SemaphoreType.DMA((2, total // HALF)),
            pltpu.SemaphoreType.DMA((2, total // HALF)),
            pltpu.SemaphoreType.DMA((1,)),
        ],
        input_output_aliases=aliases,
        compiler_params=PARAMS,
        cost_estimate=pl.CostEstimate(
            flops=2 * total * units * width,
            bytes_accessed=2 * (total * width + width * units + 4 * total * units),
            transcendentals=total * units,
        ),
        name="hidden_grads",
    )(*args)
    return outs, mark


def weight_sum_kernel(counts, lane, span, factor, waits, acc, got, *refs):
    n = len(counts)
    refs = list(refs[waits:])

    def take(k, there=True):
        return [refs.pop(0) for _ in range(k)] if there else [None] * k

    (first,) = take(1)
    rows = take(n)
    (hid,) = take(1)
    (acc_in,) = take(1, acc)
    (got_in,) = take(1, got)
    out, done, rows_s, hid_s, out_s, row_sems, sems = take(7)
    (acc_s,) = take(1, acc)
    (got_s,) = take(1, got)
    total = sum(counts)
    col0 = first[0] * COLS
    in_copies = [pltpu.make_async_copy(hid.at[:, pl.ds(lane, total)], hid_s, sems.at[3, 0])]
    for i, (at, m) in enumerate(zip(starts_of(counts), counts)):
        src = rows[i].at[:, pl.ds(pl.multiple_of(col0, COLS), span * COLS)]
        in_copies.append(pltpu.make_async_copy(src, rows_s.at[pl.ds(at, m)], row_sems.at[i]))
    acc_copies, got_copies, out_copies = [], [], []
    for j in range(span):
        here = pl.ds(j * COLS, COLS)
        if acc:
            there = pl.ds(pl.multiple_of(col0 + j * COLS, COLS), COLS)
            acc_copies.append(pltpu.make_async_copy(acc_in.at[:, there], acc_s.at[j], sems.at[0, j]))
        if got:
            got_copies.append(pltpu.make_async_copy(got_in.at[:, here], got_s.at[j], sems.at[2, j]))
        out_copies.append(pltpu.make_async_copy(out_s.at[j], out.at[:, here], sems.at[1, j]))
    for c in in_copies + acc_copies + got_copies:
        c.start()
    for c in in_copies:
        c.wait()
    for j in range(span):
        part = jnp.dot(hid_s[...], rows_s[:, pl.ds(j * COLS, COLS)], preferred_element_type=jnp.float32)
        if acc:
            acc_copies[j].wait()
            part = acc_s[j] + part
        if got:
            got_copies[j].wait()
            part = part + got_s[j].astype(jnp.float32)
        if factor:
            part = part * factor
        out_s[j] = part.astype(out_s.dtype)
        out_copies[j].start()
    done[0] = 0
    for c in out_copies:
        c.wait()


def weight_sums(parts, hid, lane, kind, *marks, acc=None, got=None, first=None, factor=None):
    rows = [p[0] for p in parts]
    counts = tuple(r.shape[0] for r in rows)
    total, n, waits = sum(counts), len(rows), len(marks)
    units, width = hid.shape[0], rows[0].shape[1]
    span = width // COLS // (1 if first is None else 2)
    first = jnp.zeros((1,), jnp.int32) if first is None else first
    args = [*marks, first, *rows, hid]
    scratch = [
        pltpu.VMEM((total, span * COLS), jnp.bfloat16),
        pltpu.VMEM((units, total), jnp.bfloat16),
        pltpu.VMEM((span, units, COLS), kind),
        pltpu.SemaphoreType.DMA((n,)),
        pltpu.SemaphoreType.DMA((4, span)),
    ]
    for a in (acc, got):
        if a is not None:
            args.append(a)
            scratch.append(pltpu.VMEM((span, units, COLS), a.dtype))
    return pl.pallas_call(
        functools.partial(
            weight_sum_kernel, counts, lane, span, factor, waits, acc is not None, got is not None
        ),
        out_shape=(jax.ShapeDtypeStruct((units, span * COLS), kind), MARK),
        in_specs=[SMEM_SPEC] * (waits + 1) + [ANY_SPEC] * (len(args) - waits - 1),
        out_specs=(ANY_SPEC, SMEM_SPEC),
        scratch_shapes=scratch,
        compiler_params=PARAMS,
        cost_estimate=pl.CostEstimate(
            flops=2 * total * units * span * COLS,
            bytes_accessed=2 * total * (units + span * COLS) + 4 * units * span * COLS,
            transcendentals=0,
        ),
        name="weight_sums",
    )(*args)


def after_kernel(*refs):
    del refs


def after(arrays, *marks):
    n = len(arrays)
    return list(pl.pallas_call(
        after_kernel,
        out_shape=tuple(jax.ShapeDtypeStruct(a.shape, a.dtype) for a in arrays),
        in_specs=[pl.BlockSpec(memory_space=pltpu.HBM)] * (n + len(marks)),
        out_specs=(pl.BlockSpec(memory_space=pltpu.HBM),) * n,
        input_output_aliases={i: i for i in range(n)},
        compiler_params=PARAMS,
        cost_estimate=pl.CostEstimate(flops=0, bytes_accessed=0, transcendentals=0),
        name="after",
    )(*arrays, *marks))


def pack_kernel(plan, n, inner, *refs):
    ins, outs, sems = refs[:n], refs[-1 - len(plan):-1], refs[-1]

    def copy(pick):
        copies = []
        for ref, blocks in zip(outs, plan):
            to = 0
            for m, *choice in blocks:
                src, at = choice[min(pick, len(choice) - 1)]
                src = ins[src].at[pl.ds(at, m)]
                copies.append(pltpu.make_async_copy(src, ref.at[pl.ds(to, m)], sems.at[len(copies)]))
                copies[-1].start()
                to += m
        for c in copies:
            c.wait()

    @pl.when(inner[0] == 1)
    def _():
        copy(0)

    @pl.when(inner[0] == 0)
    def _():
        copy(1)


def pack(inner, arrays, plan, *marks):
    width = arrays[0].shape[1]
    sizes = [sum(b[0] for b in blocks) for blocks in plan]
    return pl.pallas_call(
        functools.partial(pack_kernel, plan, len(arrays)),
        out_shape=tuple(jax.ShapeDtypeStruct((m, width), jnp.bfloat16) for m in sizes),
        in_specs=[SMEM_SPEC] + [ANY_SPEC] * (len(arrays) + len(marks)),
        out_specs=(pl.BlockSpec(memory_space=pltpu.VMEM),) * len(plan),
        scratch_shapes=[pltpu.SemaphoreType.DMA((sum(len(b) for b in plan),))],
        compiler_params=PARAMS,
        cost_estimate=pl.CostEstimate(flops=0, bytes_accessed=4 * sum(sizes) * width, transcendentals=0),
        name="pack",
    )(inner, *arrays, *marks)


def per_device(cotangent, scales, routes, gate, up, weight):
    dp = lax.axis_index("dp")
    expert = lax.axis_index("expert")
    tensor = lax.axis_index("tensor")
    x, zhi = expert & 3, expert >> 2
    y, z = tensor >> 2, tensor & 3
    gate, up, weight = gate[0, 0], up[0, 0], weight[0]
    inner = ((z == 1) | (z == 2)).astype(jnp.int32).reshape(1)

    wt = weight.T
    place = jnp.stack([x, zhi]).astype(jnp.int32)
    blocks = list(dispatch(place, cotangent[0], scales, routes))
    u_own, v1, v2 = assemble(place, blocks[:1] + [send(blocks[k], X_STEP[k]) for k in range(1, NX)], wt)

    far1 = jnp.where(z < 2, 2, 1)
    far2 = jnp.where(z < 2, 3, 0)

    s = 1 - 2 * dp
    wa, wn = [(0, z)], [(0, z ^ 1)]
    wb, wc, wd = [(1, z), (0, far1)], [(1, z ^ 1), (0, far2)], [(1, far1), (1, far2)]
    order = []

    def parts_of(arrays, what, ys):
        parts = []
        for a, yy in zip(arrays, ys):
            ids = []
            for kind, zz in what:
                src, hi = (zz, zhi) if kind == 0 else (NZ - 1 - zz, 1 - zhi)
                ids.append(len(order))
                order.append(((yy & 3) * NZ + src) * (2 * HALF) + hi * HALF)
            parts.append((a, tuple(ids)))
        return parts

    def ring(own):
        return [own, send(own, Y_ON), send(own, Y_BACK)]

    y3, y4 = [y, y - s, y + s], [y - 2 * s]
    theirs = ((1 - dp) * 3).astype(jnp.int32).reshape(1)
    mine = (dp * 3).astype(jnp.int32).reshape(1)

    v1 = send(v1, Z_MIRROR)
    a = ring(u_own)
    u_near = send(u_own, Z_PAIR)
    u_mid1 = send(u_own, Z_MIDDLE)
    u_near, u_mid1 = after([u_near, u_mid1], v1, *a[1:])
    v2 = send(v2, Z_MIRROR)
    n = ring(u_near)
    u_mid2 = send(u_near, Z_MIDDLE)
    u_out1 = send(u_mid1, Z_PAIR)
    an = parts_of(a, wa, y3) + parts_of(n, wn, y3)
    an4 = parts_of([None], wa + wn, y4)
    b3, b4 = parts_of([None] * 3, wb, y3), parts_of([None], wb, y4)
    c3, c4 = parts_of([None] * 3, wc, y3), parts_of([None], wc, y4)
    d3, d4 = parts_of([None] * 3, wd, y3), parts_of([None], wd, y4)
    offs = jnp.stack(order).astype(jnp.int32)

    def fill(parts, arrays):
        return [(a, p[1]) for a, p in zip(arrays, parts)]

    hid, h = hidden_rows(offs, gate, up)
    b_own, x3, v_own, on4 = pack(
        inner, [v1, v2, u_mid1, u_out1, u_mid2, a[1], n[1]],
        (
            ((32, (0, 0)), (32, (1, 0)), (64, (2, 0), (3, 0))),
            ((32, (0, 0)), (32, (1, 0)), (64, (4, 0))),
            ((32, (0, 0)), (32, (1, 0))),
            ((64, (5, 0)), (64, (6, 0))),
        ),
        h, n[2],
    )
    pair3 = send(x3, Z_PAIR)
    mid3 = send(v_own, Z_MIDDLE)
    b = ring(b_own)
    an4 = fill(an4, [send(on4, Y_ON)])
    outs, m1 = hidden_grads(an, offs, gate, up, wt, None)
    c_own, v_near = pack(
        inner, [pair3, x3],
        (((64, (0, 0)), (64, (1, 64), (0, 64))), ((64, (0, 0)),)),
        m1, b[1],
    )
    mid4 = send(v_near, Z_MIDDLE)
    pair4 = send(mid3, Z_PAIR)
    c = ring(c_own)
    b3, b4 = fill(b3, b), fill(b4, [send(b[1], Y_ON)])
    pair5 = send(mid4, Z_PAIR)
    outs, m2 = hidden_grads(an4 + b3, offs, gate, up, wt, outs, m1)
    acc, m3 = weight_sums(an + an4 + b3, hid, 0, jnp.float32, m2)
    (d_own,) = pack(
        inner, [mid3, pair4, mid4, pair5],
        (((64, (0, 0), (1, 0)), (64, (2, 0), (3, 0))),),
        m3, c[1],
    )
    c3, c4 = fill(c3, c), fill(c4, [send(c[1], Y_ON)])
    d = ring(d_own)
    outs, m4 = hidden_grads(b4 + c3, offs, gate, up, wt, outs, m3)
    acc, m5 = weight_sums(b4 + c3, hid, 14 * HALF, jnp.float32, m4, acc=acc)
    d[1], = after([d[1]], m5)
    d3, d4 = fill(d3, d), fill(d4, [send(d[1], Y_ON)])
    outs, m6 = hidden_grads(c4 + d3, offs, gate, up, wt, outs, m5)
    rest, lane = c4 + d3 + d4, 22 * HALF
    give, m7 = weight_sums(rest, hid, lane, jnp.bfloat16, m6, acc=acc, first=theirs)
    got = send(give, DP_SWAP)
    outs, m8 = hidden_grads(d4, offs, gate, up, wt, outs, m7)
    factor = 1.0 / (2 * 64 * 8 * 16) ** 0.5
    weight_grad, _ = weight_sums(
        rest, hid, lane, jnp.bfloat16, m8, acc=acc, got=got, first=mine, factor=factor
    )
    return (outs[0][None, None], outs[1][None, None], weight_grad[None])


def solution(mesh):
    in_specs = (
        P("dp", ("expert", "tensor"), None),
        P("dp", ("expert", "tensor")),
        P("dp", ("expert", "tensor"), None),
        P("dp", "expert", None, "tensor"),
        P("dp", "expert", None, "tensor"),
        P("expert", "tensor", None),
    )
    out_specs = (
        P("dp", "expert", None, "tensor"),
        P("dp", "expert", None, "tensor"),
        P("expert", "tensor", "dp"),
    )
    return jax.shard_map(
        per_device, mesh=mesh, in_specs=in_specs, out_specs=out_specs, check_vma=False
    )
```

```python
import functools

import jax
import jax.numpy as jnp
from jax import lax
from jax.experimental import pallas as pl
from jax.experimental.pallas import tpu as pltpu
from jax.sharding import PartitionSpec as P

AX = ("dp", "expert", "tensor")
NX, NY, NZ = 4, 4, 4
SLOT = 16
HALF = NX * SLOT
ANY = pl.ANY
VMEM_LIMIT = 20 * 1024 * 1024
PARAMS = pltpu.CompilerParams(vmem_limit_bytes=VMEM_LIMIT)
WHOLE = pltpu.CompilerParams(vmem_limit_bytes=62 * 1024 * 1024)


def chip_perm(fn):
    pairs = []
    for c in range(2):
        for z in range(2 * NZ):
            for x in range(NX):
                for y in range(NY):
                    to = fn(c, x, y, z)
                    if to is not None:
                        pairs.append((flat(c, x, y, z), flat(*to)))
    return pairs


def flat(c, x, y, z):
    x, y, z = x % NX, y % NY, z % (2 * NZ)
    return (c * 2 * NX + (z // NZ) * NX + x) * NY * NZ + y * NZ + z % NZ


X_STEP = [chip_perm(lambda c, x, y, z, k=k: (c, x + k, y, z)) for k in range(NX)]
Y_ON = chip_perm(lambda c, x, y, z: (c, x, y + 1 - 2 * c, z))
Y_BACK = chip_perm(lambda c, x, y, z: (c, x, y - 1 + 2 * c, z))
Z_MIRROR = chip_perm(lambda c, x, y, z: (c, x, y, 2 * NZ - 1 - z))
Z_PAIR = chip_perm(lambda c, x, y, z: (c, x, y, z ^ 1))
Z_MIDDLE = chip_perm(lambda c, x, y, z: (c, x, y, z ^ 3) if z % NZ in (1, 2) else None)
DP_SWAP = chip_perm(lambda c, x, y, z: (1 - c, x, y, z))


def send(a, pairs):
    return lax.ppermute(a, AX, pairs)


def dispatch_kernel(place, cot, scales, ids, *outs):
    tok = cot.shape[0]
    x, zhi = place[0], place[1]
    above = lax.broadcasted_iota(jnp.int32, (tok, tok), 0)
    along = lax.broadcasted_iota(jnp.int32, (tok, tok), 1)
    row = jnp.broadcast_to(ids[...], (tok, tok))
    eye = above == along
    col = jnp.sum(jnp.where(eye, row, 0).astype(jnp.float32), axis=1, keepdims=True)
    col = jnp.broadcast_to(col, (tok, tok)).astype(jnp.int32)
    same = jnp.where((col == row) & (above < along), 1.0, 0.0)
    slot = jnp.sum(same, axis=0, keepdims=True).astype(jnp.int32)
    row = ids[...]
    other = jnp.where((row >> 2) == zhi, 0, SLOT)
    target = ((row - x) & (NX - 1)) * (2 * SLOT) + other + slot
    pick = lax.broadcasted_iota(jnp.int32, (2 * HALF, tok), 0) == target
    pick = jnp.where(pick, 1.0, 0.0).astype(jnp.bfloat16)
    scale = jnp.sum(jnp.where(eye, jnp.broadcast_to(scales[...], (tok, tok)), 0.0), axis=1, keepdims=True)
    scaled = (cot[...].astype(jnp.float32) * scale).astype(jnp.bfloat16)
    out = jnp.dot(pick, scaled, preferred_element_type=jnp.float32).astype(jnp.bfloat16)
    for k, ref in enumerate(outs):
        ref[...] = out[k * 2 * SLOT:(k + 1) * 2 * SLOT]


def dispatch(place, cot, scales, ids):
    tok, width = cot.shape
    block = jax.ShapeDtypeStruct((2 * SLOT, width), jnp.bfloat16)
    vmem = pl.BlockSpec(memory_space=pltpu.VMEM)
    return pl.pallas_call(
        dispatch_kernel,
        out_shape=(block,) * NX,
        in_specs=[pl.BlockSpec(memory_space=pltpu.SMEM)] + [vmem] * 3,
        out_specs=(vmem,) * NX,
        compiler_params=PARAMS,
        name="dispatch",
    )(place, cot, scales, ids.reshape(1, tok))


def assemble_kernel(place, b0, b1, b2, b3, mark, u, v1, v2, v_s):
    del mark
    x = place[0]
    for k, ref in enumerate((b0, b1, b2, b3)):
        at = pl.multiple_of(((x - k) & (NX - 1)) * SLOT, SLOT)
        u[pl.ds(at, SLOT), :] = ref[:SLOT]
        v_s[pl.ds(at, SLOT), :] = ref[SLOT:]
    v1[...] = v_s[:HALF // 2]
    v2[...] = v_s[HALF // 2:]


def assemble(place, blocks, mark):
    width = blocks[0].shape[1]
    vmem = pl.BlockSpec(memory_space=pltpu.VMEM)
    return pl.pallas_call(
        assemble_kernel,
        out_shape=tuple(jax.ShapeDtypeStruct((m, width), jnp.bfloat16) for m in (HALF, HALF // 2, HALF // 2)),
        in_specs=[pl.BlockSpec(memory_space=pltpu.SMEM)] + [vmem] * NX + [pl.BlockSpec(memory_space=ANY)],
        out_specs=(vmem,) * 3,
        scratch_shapes=[pltpu.VMEM((HALF, width), jnp.bfloat16)],
        compiler_params=PARAMS,
        name="assemble",
    )(place, *blocks, mark)


def starts_of(sizes):
    at = [0]
    for m in sizes:
        at.append(at[-1] + m)
    return at


COLS = 512
SMEM_SPEC = pl.BlockSpec(memory_space=pltpu.SMEM)
ANY_SPEC = pl.BlockSpec(memory_space=ANY)
HBM_SPEC = pl.BlockSpec(memory_space=pltpu.HBM)
MARK = jax.ShapeDtypeStruct((1,), jnp.int32)


def hidden_kernel(offs, gate, up, hid_t, done, hid_s):
    blocks = hid_t.shape[1] // HALF
    for b in range(0, blocks, 2):
        for i in range(2):
            there = pl.ds(pl.multiple_of(offs[b + i], HALF), HALF)
            g = gate[there, :].astype(jnp.float32)
            u = up[there, :].astype(jnp.float32)
            hid_s[pl.ds(i * HALF, HALF), :] = (g * jax.nn.sigmoid(g) * u).astype(jnp.bfloat16)
        hid_t[:, pl.ds(b * HALF, 2 * HALF)] = hid_s[...].T
    done[0] = 0


def hidden_rows(offs, gate, up):
    slots, units = gate.shape
    vmem = pl.BlockSpec(memory_space=pltpu.VMEM)
    return pl.pallas_call(
        hidden_kernel,
        out_shape=(jax.ShapeDtypeStruct((units, slots), jnp.bfloat16), MARK),
        in_specs=[SMEM_SPEC, vmem, vmem],
        out_specs=(vmem, SMEM_SPEC),
        scratch_shapes=[pltpu.VMEM((2 * HALF, units), jnp.bfloat16)],
        compiler_params=PARAMS,
        cost_estimate=pl.CostEstimate(
            flops=0, bytes_accessed=6 * slots * units, transcendentals=slots * units
        ),
        name="hidden_rows",
    )(offs, gate, up)


def hidden_grad_kernel(counts, ids, waits, outs, *refs):
    n = len(counts)
    refs = list(refs[waits:])

    def take(k, there=True):
        return [refs.pop(0) for _ in range(k)] if there else [None] * k

    (offs,) = take(1)
    rows = take(n)
    gate, up, wt = take(3)
    take(2, outs)
    gg, gu, done, rows_s, wt_s, gate_s, up_s, gg_s, gu_s, row_sems, in_sems, out_sems, w_sem = take(13)
    total = sum(counts)
    in_copies, out_copies = [], []
    for b in range(total // HALF):
        here = pl.ds(b * HALF, HALF)
        there = pl.ds(pl.multiple_of(offs[ids[b]], HALF), HALF)
        for k, (src, dst) in enumerate(((gate, gate_s), (up, up_s))):
            in_copies.append((b * HALF, pltpu.make_async_copy(src.at[there], dst.at[here], in_sems.at[k, b])))
            in_copies[-1][1].start()
        for k, (src, dst) in enumerate(((gg_s, gg), (gu_s, gu))):
            out_copies.append((b * HALF, pltpu.make_async_copy(src.at[here], dst.at[there], out_sems.at[k, b])))
    w_copy = pltpu.make_async_copy(wt, wt_s, w_sem.at[0])
    w_copy.start()
    for i, (at, m) in enumerate(zip(starts_of(counts), counts)):
        in_copies.append((at, pltpu.make_async_copy(rows[i], rows_s.at[pl.ds(at, m)], row_sems.at[i])))
        in_copies[-1][1].start()
    for begin in range(0, total, 256):
        end = min(begin + 256, total)
        here = pl.ds(begin, end - begin)
        for at, c in in_copies:
            if begin <= at < end:
                c.wait()
        if begin == 0:
            w_copy.wait()
        grad = jnp.dot(rows_s[here, :], wt_s[...], preferred_element_type=jnp.float32)
        g = gate_s[here, :].astype(jnp.float32)
        u = up_s[here, :].astype(jnp.float32)
        sig = jax.nn.sigmoid(g)
        gg_s[here, :] = (grad * u * sig * (1.0 + g * (1.0 - sig))).astype(jnp.bfloat16)
        gu_s[here, :] = (grad * (g * sig)).astype(jnp.bfloat16)
        for at, c in out_copies:
            if begin <= at < end:
                c.start()
    done[0] = 0
    for _, c in out_copies:
        c.wait()


def hidden_grads(parts, offs, gate, up, wt, outs, *marks, params=PARAMS):
    rows = [p[0] for p in parts]
    ids = tuple(i for p in parts for i in p[1])
    counts = tuple(r.shape[0] for r in rows)
    total, n, waits = sum(counts), len(rows), len(marks)
    width, units = wt.shape
    args = [*marks, offs, *rows, gate, up, wt]
    aliases = {}
    if outs:
        aliases = {len(args): 0, len(args) + 1: 1}
        args += list(outs)
    tile = pltpu.VMEM((total, units), jnp.bfloat16)
    *outs, mark = pl.pallas_call(
        functools.partial(hidden_grad_kernel, counts, ids, waits, bool(outs)),
        out_shape=(jax.ShapeDtypeStruct(gate.shape, jnp.bfloat16),) * 2 + (MARK,),
        in_specs=[SMEM_SPEC] * (waits + 1) + [ANY_SPEC] * (n + 3) + [HBM_SPEC] * (2 if outs else 0),
        out_specs=(HBM_SPEC, HBM_SPEC, SMEM_SPEC),
        scratch_shapes=[
            pltpu.VMEM((total, width), jnp.bfloat16),
            pltpu.VMEM((width, units), jnp.bfloat16),
            tile, tile, tile, tile,
            pltpu.SemaphoreType.DMA((n,)),
            pltpu.SemaphoreType.DMA((2, total // HALF)),
            pltpu.SemaphoreType.DMA((2, total // HALF)),
            pltpu.SemaphoreType.DMA((1,)),
        ],
        input_output_aliases=aliases,
        compiler_params=params,
        cost_estimate=pl.CostEstimate(
            flops=2 * total * units * width,
            bytes_accessed=2 * (total * width + width * units + 4 * total * units),
            transcendentals=total * units,
        ),
        name="hidden_grads",
    )(*args)
    return outs, mark


def weight_sum_kernel(counts, lane, span, factor, waits, acc, got, *refs):
    n = len(counts)
    refs = list(refs[waits:])

    def take(k, there=True):
        return [refs.pop(0) for _ in range(k)] if there else [None] * k

    (first,) = take(1)
    rows = take(n)
    (hid,) = take(1)
    (acc_in,) = take(1, acc)
    (got_in,) = take(1, got)
    out, done, rows_s, hid_s, out_s, row_sems, sems = take(7)
    (acc_s,) = take(1, acc)
    (got_s,) = take(1, got)
    total = sum(counts)
    col0 = first[0] * COLS
    in_copies = [pltpu.make_async_copy(hid.at[:, pl.ds(lane, total)], hid_s, sems.at[3, 0])]
    for i, (at, m) in enumerate(zip(starts_of(counts), counts)):
        src = rows[i].at[:, pl.ds(pl.multiple_of(col0, COLS), span * COLS)]
        in_copies.append(pltpu.make_async_copy(src, rows_s.at[pl.ds(at, m)], row_sems.at[i]))
    acc_copies, got_copies, out_copies = [], [], []
    for j in range(span):
        here = pl.ds(j * COLS, COLS)
        if acc:
            there = pl.ds(pl.multiple_of(col0 + j * COLS, COLS), COLS)
            acc_copies.append(pltpu.make_async_copy(acc_in.at[:, there], acc_s.at[j], sems.at[0, j]))
        if got:
            got_copies.append(pltpu.make_async_copy(got_in.at[:, here], got_s.at[j], sems.at[2, j]))
        out_copies.append(pltpu.make_async_copy(out_s.at[j], out.at[:, here], sems.at[1, j]))
    for c in in_copies + acc_copies + got_copies:
        c.start()
    for c in in_copies:
        c.wait()
    for j in range(span):
        part = jnp.dot(hid_s[...], rows_s[:, pl.ds(j * COLS, COLS)], preferred_element_type=jnp.float32)
        if acc:
            acc_copies[j].wait()
            part = acc_s[j] + part
        if got:
            got_copies[j].wait()
            part = part + got_s[j].astype(jnp.float32)
        if factor:
            part = part * factor
        out_s[j] = part.astype(out_s.dtype)
        out_copies[j].start()
    done[0] = 0
    for c in out_copies:
        c.wait()


def weight_sums(parts, hid, lane, kind, *marks, acc=None, got=None, first=None, factor=None, params=PARAMS):
    rows = [p[0] for p in parts]
    counts = tuple(r.shape[0] for r in rows)
    total, n, waits = sum(counts), len(rows), len(marks)
    units, width = hid.shape[0], rows[0].shape[1]
    span = width // COLS // (1 if first is None else 2)
    first = jnp.zeros((1,), jnp.int32) if first is None else first
    args = [*marks, first, *rows, hid]
    scratch = [
        pltpu.VMEM((total, span * COLS), jnp.bfloat16),
        pltpu.VMEM((units, total), jnp.bfloat16),
        pltpu.VMEM((span, units, COLS), kind),
        pltpu.SemaphoreType.DMA((n,)),
        pltpu.SemaphoreType.DMA((4, span)),
    ]
    for a in (acc, got):
        if a is not None:
            args.append(a)
            scratch.append(pltpu.VMEM((span, units, COLS), a.dtype))
    return pl.pallas_call(
        functools.partial(
            weight_sum_kernel, counts, lane, span, factor, waits, acc is not None, got is not None
        ),
        out_shape=(jax.ShapeDtypeStruct((units, span * COLS), kind), MARK),
        in_specs=[SMEM_SPEC] * (waits + 1)
        + [ANY_SPEC] * (n + 1)
        + [HBM_SPEC] * (acc is not None)
        + [ANY_SPEC] * (got is not None),
        out_specs=(HBM_SPEC, SMEM_SPEC),
        scratch_shapes=scratch,
        compiler_params=params,
        cost_estimate=pl.CostEstimate(
            flops=2 * total * units * span * COLS,
            bytes_accessed=2 * total * (units + span * COLS) + 4 * units * span * COLS,
            transcendentals=0,
        ),
        name="weight_sums",
    )(*args)


def after_kernel(*refs):
    del refs


def after(arrays, *marks):
    n = len(arrays)
    return list(pl.pallas_call(
        after_kernel,
        out_shape=tuple(jax.ShapeDtypeStruct(a.shape, a.dtype) for a in arrays),
        in_specs=[pl.BlockSpec(memory_space=pltpu.HBM)] * (n + len(marks)),
        out_specs=(pl.BlockSpec(memory_space=pltpu.HBM),) * n,
        input_output_aliases={i: i for i in range(n)},
        compiler_params=PARAMS,
        cost_estimate=pl.CostEstimate(flops=0, bytes_accessed=0, transcendentals=0),
        name="after",
    )(*arrays, *marks))


def pack_kernel(plan, n, inner, *refs):
    ins, outs, sems = refs[:n], refs[-1 - len(plan):-1], refs[-1]

    def copy(pick):
        copies = []
        for ref, blocks in zip(outs, plan):
            to = 0
            for m, *choice in blocks:
                src, at = choice[min(pick, len(choice) - 1)]
                src = ins[src].at[pl.ds(at, m)]
                copies.append(pltpu.make_async_copy(src, ref.at[pl.ds(to, m)], sems.at[len(copies)]))
                copies[-1].start()
                to += m
        for c in copies:
            c.wait()

    @pl.when(inner[0] == 1)
    def _():
        copy(0)

    @pl.when(inner[0] == 0)
    def _():
        copy(1)


def pack(inner, arrays, plan, *marks):
    width = arrays[0].shape[1]
    sizes = [sum(b[0] for b in blocks) for blocks in plan]
    return pl.pallas_call(
        functools.partial(pack_kernel, plan, len(arrays)),
        out_shape=tuple(jax.ShapeDtypeStruct((m, width), jnp.bfloat16) for m in sizes),
        in_specs=[SMEM_SPEC] + [ANY_SPEC] * (len(arrays) + len(marks)),
        out_specs=(pl.BlockSpec(memory_space=pltpu.VMEM),) * len(plan),
        scratch_shapes=[pltpu.SemaphoreType.DMA((sum(len(b) for b in plan),))],
        compiler_params=PARAMS,
        cost_estimate=pl.CostEstimate(flops=0, bytes_accessed=4 * sum(sizes) * width, transcendentals=0),
        name="pack",
    )(inner, *arrays, *marks)


def per_device(cotangent, scales, routes, gate, up, weight):
    dp = lax.axis_index("dp")
    expert = lax.axis_index("expert")
    tensor = lax.axis_index("tensor")
    x, zhi = expert & 3, expert >> 2
    y, z = tensor >> 2, tensor & 3
    gate, up, weight = gate[0, 0], up[0, 0], weight[0]
    inner = ((z == 1) | (z == 2)).astype(jnp.int32).reshape(1)

    wt = weight.T
    place = jnp.stack([x, zhi]).astype(jnp.int32)
    blocks = list(dispatch(place, cotangent[0], scales, routes))
    u_own, v1, v2 = assemble(place, blocks[:1] + [send(blocks[k], X_STEP[k]) for k in range(1, NX)], wt)

    far1 = jnp.where(z < 2, 2, 1)
    far2 = jnp.where(z < 2, 3, 0)

    s = 1 - 2 * dp
    wa, wn = [(0, z)], [(0, z ^ 1)]
    wb, wc, wd = [(1, z), (0, far1)], [(1, z ^ 1), (0, far2)], [(1, far1), (1, far2)]
    order = []

    def parts_of(arrays, what, ys):
        parts = []
        for a, yy in zip(arrays, ys):
            ids = []
            for kind, zz in what:
                src, hi = (zz, zhi) if kind == 0 else (NZ - 1 - zz, 1 - zhi)
                ids.append(len(order))
                order.append(((yy & 3) * NZ + src) * (2 * HALF) + hi * HALF)
            parts.append((a, tuple(ids)))
        return parts

    def ring(own):
        return [own, send(own, Y_ON), send(own, Y_BACK)]

    y3, y4 = [y, y - s, y + s], [y - 2 * s]
    theirs = ((1 - dp) * 3).astype(jnp.int32).reshape(1)
    mine = (dp * 3).astype(jnp.int32).reshape(1)

    v1 = send(v1, Z_MIRROR)
    a = ring(u_own)
    u_near = send(u_own, Z_PAIR)
    u_mid1 = send(u_own, Z_MIDDLE)
    u_near, u_mid1 = after([u_near, u_mid1], v1, *a[1:])
    v2 = send(v2, Z_MIRROR)
    n = ring(u_near)
    u_mid2 = send(u_near, Z_MIDDLE)
    u_out1 = send(u_mid1, Z_PAIR)
    an = parts_of(a, wa, y3) + parts_of(n, wn, y3)
    an4 = parts_of([None], wa + wn, y4)
    b3, b4 = parts_of([None] * 3, wb, y3), parts_of([None], wb, y4)
    c3, c4 = parts_of([None] * 3, wc, y3), parts_of([None], wc, y4)
    d3, d4 = parts_of([None] * 3, wd, y3), parts_of([None], wd, y4)
    offs = jnp.stack(order).astype(jnp.int32)

    def fill(parts, arrays):
        return [(a, p[1]) for a, p in zip(arrays, parts)]

    hid, h = hidden_rows(offs, gate, up)
    b_own, x3, v_own, on4 = pack(
        inner, [v1, v2, u_mid1, u_out1, u_mid2, a[1], n[1]],
        (
            ((32, (0, 0)), (32, (1, 0)), (64, (2, 0), (3, 0))),
            ((32, (0, 0)), (32, (1, 0)), (64, (4, 0))),
            ((32, (0, 0)), (32, (1, 0))),
            ((64, (5, 0)), (64, (6, 0))),
        ),
        h, n[2],
    )
    pair3 = send(x3, Z_PAIR)
    mid3 = send(v_own, Z_MIDDLE)
    b = ring(b_own)
    an4 = fill(an4, [send(on4, Y_ON)])
    outs, m1 = hidden_grads(an, offs, gate, up, wt, None)
    c_own, v_near = pack(
        inner, [pair3, x3],
        (((64, (0, 0)), (64, (1, 64), (0, 64))), ((64, (0, 0)),)),
        m1, b[1],
    )
    mid4 = send(v_near, Z_MIDDLE)
    pair4 = send(mid3, Z_PAIR)
    c = ring(c_own)
    b3, b4 = fill(b3, b), fill(b4, [send(b[1], Y_ON)])
    pair5 = send(mid4, Z_PAIR)
    outs, m2 = hidden_grads(an4 + b3, offs, gate, up, wt, outs, m1)
    acc, m3 = weight_sums(an + an4 + b3, hid, 0, jnp.float32, m2)
    (d_own,) = pack(
        inner, [mid3, pair4, mid4, pair5],
        (((64, (0, 0), (1, 0)), (64, (2, 0), (3, 0))),),
        m3, c[1],
    )
    c3, c4 = fill(c3, c), fill(c4, [send(c[1], Y_ON)])
    d = ring(d_own)
    outs, m4 = hidden_grads(b4 + c3, offs, gate, up, wt, outs, m3)
    acc, m5 = weight_sums(b4 + c3, hid, 14 * HALF, jnp.float32, m4, acc=acc)
    d[1], = after([d[1]], m5)
    d3, d4 = fill(d3, d), fill(d4, [send(d[1], Y_ON)])
    outs, m6 = hidden_grads(c4 + d3, offs, gate, up, wt, outs, m5, params=WHOLE)
    rest, lane = c4 + d3 + d4, 22 * HALF
    give, m7 = weight_sums(rest, hid, lane, jnp.bfloat16, m6, acc=acc, first=theirs, params=WHOLE)
    got = send(give, DP_SWAP)
    outs, m8 = hidden_grads(d4, offs, gate, up, wt, outs, m7, params=WHOLE)
    factor = 1.0 / (2 * 64 * 8 * 16) ** 0.5
    weight_grad, _ = weight_sums(
        rest, hid, lane, jnp.bfloat16, m8, acc=acc, got=got, first=mine, factor=factor, params=WHOLE
    )
    return (outs[0][None, None], outs[1][None, None], weight_grad[None])


def solution(mesh):
    in_specs = (
        P("dp", ("expert", "tensor"), None),
        P("dp", ("expert", "tensor")),
        P("dp", ("expert", "tensor"), None),
        P("dp", "expert", None, "tensor"),
        P("dp", "expert", None, "tensor"),
        P("expert", "tensor", None),
    )
    out_specs = (
        P("dp", "expert", None, "tensor"),
        P("dp", "expert", None, "tensor"),
        P("expert", "tensor", "dp"),
    )
    return jax.shard_map(
        per_device, mesh=mesh, in_specs=in_specs, out_specs=out_specs, check_vma=False
    )
```

```python
import functools

import jax
import jax.numpy as jnp
from jax import lax
from jax.experimental import pallas as pl
from jax.experimental.pallas import tpu as pltpu
from jax.sharding import PartitionSpec as P

AX = ("dp", "expert", "tensor")
NX, NY, NZ = 4, 4, 4
SLOT = 16
HALF = NX * SLOT
ANY = pl.ANY
VMEM_LIMIT = 20 * 1024 * 1024
PARAMS = pltpu.CompilerParams(vmem_limit_bytes=VMEM_LIMIT)
WHOLE = pltpu.CompilerParams(vmem_limit_bytes=62 * 1024 * 1024)


def chip_perm(fn):
    pairs = []
    for c in range(2):
        for z in range(2 * NZ):
            for x in range(NX):
                for y in range(NY):
                    to = fn(c, x, y, z)
                    if to is not None:
                        pairs.append((flat(c, x, y, z), flat(*to)))
    return pairs


def flat(c, x, y, z):
    x, y, z = x % NX, y % NY, z % (2 * NZ)
    return (c * 2 * NX + (z // NZ) * NX + x) * NY * NZ + y * NZ + z % NZ


X_STEP = [chip_perm(lambda c, x, y, z, k=k: (c, x + k, y, z)) for k in range(NX)]
Y_ON = chip_perm(lambda c, x, y, z: (c, x, y + 1 - 2 * c, z))
Y_BACK = chip_perm(lambda c, x, y, z: (c, x, y - 1 + 2 * c, z))
Z_MIRROR = chip_perm(lambda c, x, y, z: (c, x, y, 2 * NZ - 1 - z))
Z_PAIR = chip_perm(lambda c, x, y, z: (c, x, y, z ^ 1))
Z_MIDDLE = chip_perm(lambda c, x, y, z: (c, x, y, z ^ 3) if z % NZ in (1, 2) else None)
DP_SWAP = chip_perm(lambda c, x, y, z: (1 - c, x, y, z))


def send(a, pairs):
    return lax.ppermute(a, AX, pairs)


def dispatch_kernel(my_x, my_zhi, cot, scales, ids, *outs):
    tok = cot.shape[0]
    x, zhi = my_x[0], my_zhi[0]
    above = lax.broadcasted_iota(jnp.int32, (tok, tok), 0)
    along = lax.broadcasted_iota(jnp.int32, (tok, tok), 1)
    row = jnp.broadcast_to(ids[...], (tok, tok))
    eye = above == along
    col = jnp.sum(jnp.where(eye, row, 0).astype(jnp.float32), axis=1, keepdims=True)
    col = jnp.broadcast_to(col, (tok, tok)).astype(jnp.int32)
    same = jnp.where((col == row) & (above < along), 1.0, 0.0)
    slot = jnp.sum(same, axis=0, keepdims=True).astype(jnp.int32)
    row = ids[...]
    other = jnp.where((row >> 2) == zhi, 0, SLOT)
    target = ((row - x) & (NX - 1)) * (2 * SLOT) + other + slot
    pick = lax.broadcasted_iota(jnp.int32, (2 * HALF, tok), 0) == target
    pick = jnp.where(pick, 1.0, 0.0).astype(jnp.bfloat16)
    scale = jnp.sum(jnp.where(eye, jnp.broadcast_to(scales[...], (tok, tok)), 0.0), axis=1, keepdims=True)
    scaled = (cot[...].astype(jnp.float32) * scale).astype(jnp.bfloat16)
    out = jnp.dot(pick, scaled, preferred_element_type=jnp.float32).astype(jnp.bfloat16)
    for k, ref in enumerate(outs):
        ref[...] = out[k * 2 * SLOT:(k + 1) * 2 * SLOT]


def dispatch(x, zhi, cot, scales, ids):
    tok, width = cot.shape
    block = jax.ShapeDtypeStruct((2 * SLOT, width), jnp.bfloat16)
    vmem = pl.BlockSpec(memory_space=pltpu.VMEM)
    return pl.pallas_call(
        dispatch_kernel,
        out_shape=(block,) * NX,
        in_specs=[pl.BlockSpec(memory_space=pltpu.SMEM)] * 2 + [vmem] * 3,
        out_specs=(vmem,) * NX,
        compiler_params=WHOLE,
        name="dispatch",
    )(x, zhi, cot, scales, ids.reshape(1, tok))


def assemble_kernel(my_x, b0, b1, b2, b3, mark, u, v1, v2, v_s):
    del mark
    x = my_x[0]
    for k, ref in enumerate((b0, b1, b2, b3)):
        at = pl.multiple_of(((x - k) & (NX - 1)) * SLOT, SLOT)
        u[pl.ds(at, SLOT), :] = ref[:SLOT]
        v_s[pl.ds(at, SLOT), :] = ref[SLOT:]
    v1[...] = v_s[:HALF // 2]
    v2[...] = v_s[HALF // 2:]


def assemble(x, blocks, mark):
    width = blocks[0].shape[1]
    vmem = pl.BlockSpec(memory_space=pltpu.VMEM)
    return pl.pallas_call(
        assemble_kernel,
        out_shape=tuple(jax.ShapeDtypeStruct((m, width), jnp.bfloat16) for m in (HALF, HALF // 2, HALF // 2)),
        in_specs=[pl.BlockSpec(memory_space=pltpu.SMEM)] + [vmem] * NX + [pl.BlockSpec(memory_space=ANY)],
        out_specs=(vmem,) * 3,
        scratch_shapes=[pltpu.VMEM((HALF, width), jnp.bfloat16)],
        compiler_params=PARAMS,
        name="assemble",
    )(x, *blocks, mark)


def starts_of(sizes):
    at = [0]
    for m in sizes:
        at.append(at[-1] + m)
    return at


COLS = 512
SMEM_SPEC = pl.BlockSpec(memory_space=pltpu.SMEM)
ANY_SPEC = pl.BlockSpec(memory_space=ANY)
HBM_SPEC = pl.BlockSpec(memory_space=pltpu.HBM)
MARK = jax.ShapeDtypeStruct((1,), jnp.int32)


def hidden_kernel(offs, gate, up, hid_t, done, hid_s):
    blocks = hid_t.shape[1] // HALF
    for b in range(0, blocks, 2):
        for i in range(2):
            there = pl.ds(pl.multiple_of(offs[b + i], HALF), HALF)
            g = gate[there, :].astype(jnp.float32)
            u = up[there, :].astype(jnp.float32)
            hid_s[pl.ds(i * HALF, HALF), :] = (g * jax.nn.sigmoid(g) * u).astype(jnp.bfloat16)
        hid_t[:, pl.ds(b * HALF, 2 * HALF)] = hid_s[...].T
    done[0] = 0


def hidden_rows(offs, gate, up):
    slots, units = gate.shape
    vmem = pl.BlockSpec(memory_space=pltpu.VMEM)
    return pl.pallas_call(
        hidden_kernel,
        out_shape=(jax.ShapeDtypeStruct((units, slots), jnp.bfloat16), MARK),
        in_specs=[SMEM_SPEC, vmem, vmem],
        out_specs=(vmem, SMEM_SPEC),
        scratch_shapes=[pltpu.VMEM((2 * HALF, units), jnp.bfloat16)],
        compiler_params=PARAMS,
        cost_estimate=pl.CostEstimate(
            flops=0, bytes_accessed=6 * slots * units, transcendentals=slots * units
        ),
        name="hidden_rows",
    )(offs, gate, up)


def hidden_grad_kernel(counts, ids, waits, outs, *refs):
    n = len(counts)
    refs = list(refs[waits:])

    def take(k, there=True):
        return [refs.pop(0) for _ in range(k)] if there else [None] * k

    (offs,) = take(1)
    rows = take(n)
    gate, up, wt = take(3)
    take(2, outs)
    gg, gu, done, rows_s, wt_s, gate_s, up_s, gg_s, gu_s, row_sems, in_sems, out_sems, w_sem = take(13)
    total = sum(counts)
    in_copies, out_copies = [], []
    for b in range(total // HALF):
        here = pl.ds(b * HALF, HALF)
        there = pl.ds(pl.multiple_of(offs[ids[b]], HALF), HALF)
        for k, (src, dst) in enumerate(((gate, gate_s), (up, up_s))):
            in_copies.append((b * HALF, pltpu.make_async_copy(src.at[there], dst.at[here], in_sems.at[k, b])))
            in_copies[-1][1].start()
        for k, (src, dst) in enumerate(((gg_s, gg), (gu_s, gu))):
            out_copies.append((b * HALF, pltpu.make_async_copy(src.at[here], dst.at[there], out_sems.at[k, b])))
    w_copy = pltpu.make_async_copy(wt, wt_s, w_sem.at[0])
    w_copy.start()
    for i, (at, m) in enumerate(zip(starts_of(counts), counts)):
        in_copies.append((at, pltpu.make_async_copy(rows[i], rows_s.at[pl.ds(at, m)], row_sems.at[i])))
        in_copies[-1][1].start()
    for begin in range(0, total, 256):
        end = min(begin + 256, total)
        here = pl.ds(begin, end - begin)
        for at, c in in_copies:
            if begin <= at < end:
                c.wait()
        if begin == 0:
            w_copy.wait()
        grad = jnp.dot(rows_s[here, :], wt_s[...], preferred_element_type=jnp.float32)
        g = gate_s[here, :].astype(jnp.float32)
        u = up_s[here, :].astype(jnp.float32)
        sig = jax.nn.sigmoid(g)
        gg_s[here, :] = (grad * u * sig * (1.0 + g * (1.0 - sig))).astype(jnp.bfloat16)
        gu_s[here, :] = (grad * (g * sig)).astype(jnp.bfloat16)
        for at, c in out_copies:
            if begin <= at < end:
                c.start()
    done[0] = 0
    for _, c in out_copies:
        c.wait()


def hidden_grads(parts, offs, gate, up, wt, outs, *marks, params=PARAMS):
    rows = [p[0] for p in parts]
    ids = tuple(i for p in parts for i in p[1])
    counts = tuple(r.shape[0] for r in rows)
    total, n, waits = sum(counts), len(rows), len(marks)
    width, units = wt.shape
    args = [*marks, offs, *rows, gate, up, wt]
    aliases = {}
    if outs:
        aliases = {len(args): 0, len(args) + 1: 1}
        args += list(outs)
    tile = pltpu.VMEM((total, units), jnp.bfloat16)
    *outs, mark = pl.pallas_call(
        functools.partial(hidden_grad_kernel, counts, ids, waits, bool(outs)),
        out_shape=(jax.ShapeDtypeStruct(gate.shape, jnp.bfloat16),) * 2 + (MARK,),
        in_specs=[SMEM_SPEC] * (waits + 1) + [ANY_SPEC] * (n + 3) + [HBM_SPEC] * (2 if outs else 0),
        out_specs=(HBM_SPEC, HBM_SPEC, SMEM_SPEC),
        scratch_shapes=[
            pltpu.VMEM((total, width), jnp.bfloat16),
            pltpu.VMEM((width, units), jnp.bfloat16),
            tile, tile, tile, tile,
            pltpu.SemaphoreType.DMA((n,)),
            pltpu.SemaphoreType.DMA((2, total // HALF)),
            pltpu.SemaphoreType.DMA((2, total // HALF)),
            pltpu.SemaphoreType.DMA((1,)),
        ],
        input_output_aliases=aliases,
        compiler_params=params,
        cost_estimate=pl.CostEstimate(
            flops=2 * total * units * width,
            bytes_accessed=2 * (total * width + width * units + 4 * total * units),
            transcendentals=total * units,
        ),
        name="hidden_grads",
    )(*args)
    return outs, mark


def weight_sum_kernel(counts, lane, span, factor, waits, acc, got, *refs):
    n = len(counts)
    refs = list(refs[waits:])

    def take(k, there=True):
        return [refs.pop(0) for _ in range(k)] if there else [None] * k

    (first,) = take(1)
    rows = take(n)
    (hid,) = take(1)
    (acc_in,) = take(1, acc)
    (got_in,) = take(1, got)
    out, done, rows_s, hid_s, out_s, row_sems, sems = take(7)
    (acc_s,) = take(1, acc)
    (got_s,) = take(1, got)
    total = sum(counts)
    col0 = first[0] * COLS
    in_copies = [pltpu.make_async_copy(hid.at[:, pl.ds(lane, total)], hid_s, sems.at[3, 0])]
    for i, (at, m) in enumerate(zip(starts_of(counts), counts)):
        src = rows[i].at[:, pl.ds(pl.multiple_of(col0, COLS), span * COLS)]
        in_copies.append(pltpu.make_async_copy(src, rows_s.at[pl.ds(at, m)], row_sems.at[i]))
    acc_copies, got_copies, out_copies = [], [], []
    for j in range(span):
        here = pl.ds(j * COLS, COLS)
        if acc:
            there = here
            if acc_in.shape[1] > span * COLS:
                there = pl.ds(pl.multiple_of(col0 + j * COLS, COLS), COLS)
            acc_copies.append(pltpu.make_async_copy(acc_in.at[:, there], acc_s.at[j], sems.at[0, j]))
        if got:
            got_copies.append(pltpu.make_async_copy(got_in.at[:, here], got_s.at[j], sems.at[2, j]))
        out_copies.append(pltpu.make_async_copy(out_s.at[j], out.at[:, here], sems.at[1, j]))
    for c in in_copies + acc_copies + got_copies:
        c.start()
    for c in in_copies:
        c.wait()
    for j in range(span):
        part = jnp.dot(hid_s[...], rows_s[:, pl.ds(j * COLS, COLS)], preferred_element_type=jnp.float32)
        if acc:
            acc_copies[j].wait()
            part = acc_s[j] + part
        if got:
            got_copies[j].wait()
            part = part + got_s[j].astype(jnp.float32)
        if factor:
            part = part * factor
        out_s[j] = part.astype(out_s.dtype)
        out_copies[j].start()
    done[0] = 0
    for c in out_copies:
        c.wait()


def weight_sums(parts, hid, lane, kind, *marks, acc=None, got=None, first=None, factor=None, params=PARAMS):
    rows = [p[0] for p in parts]
    counts = tuple(r.shape[0] for r in rows)
    total, n, waits = sum(counts), len(rows), len(marks)
    units, width = hid.shape[0], rows[0].shape[1]
    span = width // COLS // (1 if first is None else 2)
    first = jnp.zeros((1,), jnp.int32) if first is None else first
    args = [*marks, first, *rows, hid]
    scratch = [
        pltpu.VMEM((total, span * COLS), jnp.bfloat16),
        pltpu.VMEM((units, total), jnp.bfloat16),
        pltpu.VMEM((span, units, COLS), kind),
        pltpu.SemaphoreType.DMA((n,)),
        pltpu.SemaphoreType.DMA((4, span)),
    ]
    for a in (acc, got):
        if a is not None:
            args.append(a)
            scratch.append(pltpu.VMEM((span, units, COLS), a.dtype))
    return pl.pallas_call(
        functools.partial(
            weight_sum_kernel, counts, lane, span, factor, waits, acc is not None, got is not None
        ),
        out_shape=(jax.ShapeDtypeStruct((units, span * COLS), kind), MARK),
        in_specs=[SMEM_SPEC] * (waits + 1)
        + [ANY_SPEC] * (n + 1)
        + [HBM_SPEC] * (acc is not None)
        + [ANY_SPEC] * (got is not None),
        out_specs=(HBM_SPEC, SMEM_SPEC),
        scratch_shapes=scratch,
        compiler_params=params,
        cost_estimate=pl.CostEstimate(
            flops=2 * total * units * span * COLS,
            bytes_accessed=2 * total * (units + span * COLS) + 4 * units * span * COLS,
            transcendentals=0,
        ),
        name="weight_sums",
    )(*args)


def after_kernel(*refs):
    del refs


def after(arrays, *marks):
    n = len(arrays)
    return list(pl.pallas_call(
        after_kernel,
        out_shape=tuple(jax.ShapeDtypeStruct(a.shape, a.dtype) for a in arrays),
        in_specs=[ANY_SPEC] * (n + len(marks)),
        out_specs=(ANY_SPEC,) * n,
        input_output_aliases={i: i for i in range(n)},
        compiler_params=PARAMS,
        cost_estimate=pl.CostEstimate(flops=0, bytes_accessed=0, transcendentals=0),
        name="after",
    )(*arrays, *marks))


def pack_kernel(plan, n, inner, *refs):
    ins, outs, sems = refs[:n], refs[-1 - len(plan):-1], refs[-1]

    def copy(pick):
        copies = []
        for ref, blocks in zip(outs, plan):
            to = 0
            for m, *choice in blocks:
                src, at = choice[min(pick, len(choice) - 1)]
                src = ins[src].at[pl.ds(at, m)]
                copies.append(pltpu.make_async_copy(src, ref.at[pl.ds(to, m)], sems.at[len(copies)]))
                copies[-1].start()
                to += m
        for c in copies:
            c.wait()

    @pl.when(inner[0] == 1)
    def _():
        copy(0)

    @pl.when(inner[0] == 0)
    def _():
        copy(1)


def pack(inner, arrays, plan, *marks):
    width = arrays[0].shape[1]
    sizes = [sum(b[0] for b in blocks) for blocks in plan]
    return pl.pallas_call(
        functools.partial(pack_kernel, plan, len(arrays)),
        out_shape=tuple(jax.ShapeDtypeStruct((m, width), jnp.bfloat16) for m in sizes),
        in_specs=[SMEM_SPEC] + [ANY_SPEC] * (len(arrays) + len(marks)),
        out_specs=(pl.BlockSpec(memory_space=pltpu.VMEM),) * len(plan),
        scratch_shapes=[pltpu.SemaphoreType.DMA((sum(len(b) for b in plan),))],
        compiler_params=PARAMS,
        cost_estimate=pl.CostEstimate(flops=0, bytes_accessed=4 * sum(sizes) * width, transcendentals=0),
        name="pack",
    )(inner, *arrays, *marks)


def per_device(cotangent, scales, routes, gate, up, weight):
    dp = lax.axis_index("dp")
    expert = lax.axis_index("expert")
    tensor = lax.axis_index("tensor")
    x, zhi = expert & 3, expert >> 2
    y, z = tensor >> 2, tensor & 3
    gate, up, weight = gate[0, 0], up[0, 0], weight[0]
    inner = ((z == 1) | (z == 2)).astype(jnp.int32).reshape(1)

    wt = weight.T
    at_x, at_zhi = [a.astype(jnp.int32).reshape(1) for a in (x, zhi)]
    blocks = list(dispatch(at_x, at_zhi, cotangent[0], scales, routes))
    u_own, v1, v2 = assemble(at_x, blocks[:1] + [send(blocks[k], X_STEP[k]) for k in range(1, NX)], wt)

    far1 = jnp.where(z < 2, 2, 1)
    far2 = jnp.where(z < 2, 3, 0)

    s = 1 - 2 * dp
    wa, wn = [(0, z)], [(0, z ^ 1)]
    wb, wc, wd = [(1, z), (0, far1)], [(1, z ^ 1), (0, far2)], [(1, far1), (1, far2)]
    order = []

    def parts_of(arrays, what, ys):
        parts = []
        for a, yy in zip(arrays, ys):
            ids = []
            for kind, zz in what:
                src, hi = (zz, zhi) if kind == 0 else (NZ - 1 - zz, 1 - zhi)
                ids.append(len(order))
                order.append(((yy & 3) * NZ + src) * (2 * HALF) + hi * HALF)
            parts.append((a, tuple(ids)))
        return parts

    def ring(own):
        return [own, send(own, Y_ON), send(own, Y_BACK)]

    y3, y4 = [y, y - s, y + s], [y - 2 * s]
    theirs = ((1 - dp) * 3).astype(jnp.int32).reshape(1)
    mine = (dp * 3).astype(jnp.int32).reshape(1)

    v1 = send(v1, Z_MIRROR)
    a = ring(u_own)
    u_near = send(u_own, Z_PAIR)
    u_mid1 = send(u_own, Z_MIDDLE)
    u_near, u_mid1 = after([u_near, u_mid1], v1, *a[1:])
    v2 = send(v2, Z_MIRROR)
    n = ring(u_near)
    u_mid2 = send(u_near, Z_MIDDLE)
    u_out1 = send(u_mid1, Z_PAIR)
    an = parts_of(a, wa, y3) + parts_of(n, wn, y3)
    an4 = parts_of([None], wa + wn, y4)
    b3, b4 = parts_of([None] * 3, wb, y3), parts_of([None], wb, y4)
    c3, c4 = parts_of([None] * 3, wc, y3), parts_of([None], wc, y4)
    d3, d4 = parts_of([None] * 3, wd, y3), parts_of([None], wd, y4)
    offs = jnp.stack(order).astype(jnp.int32)

    def fill(parts, arrays):
        return [(a, p[1]) for a, p in zip(arrays, parts)]

    hid, h = hidden_rows(offs, gate, up)
    b_own, x3, v_own, on4 = pack(
        inner, [v1, v2, u_mid1, u_out1, u_mid2, a[1], n[1]],
        (
            ((32, (0, 0)), (32, (1, 0)), (64, (2, 0), (3, 0))),
            ((32, (0, 0)), (32, (1, 0)), (64, (4, 0))),
            ((32, (0, 0)), (32, (1, 0))),
            ((64, (5, 0)), (64, (6, 0))),
        ),
        h, n[2],
    )
    pair3 = send(x3, Z_PAIR)
    mid3 = send(v_own, Z_MIDDLE)
    b = ring(b_own)
    an4 = fill(an4, [send(on4, Y_ON)])
    outs, m1 = hidden_grads(an, offs, gate, up, wt, None)
    c_own, v_near = pack(
        inner, [pair3, x3],
        (((64, (0, 0)), (64, (1, 64), (0, 64))), ((64, (0, 0)),)),
        m1, b[1],
    )
    mid4 = send(v_near, Z_MIDDLE)
    pair4 = send(mid3, Z_PAIR)
    c = ring(c_own)
    b3, b4 = fill(b3, b), fill(b4, [send(b[1], Y_ON)])
    pair5 = send(mid4, Z_PAIR)
    outs, m2 = hidden_grads(an4 + b3, offs, gate, up, wt, outs, m1)
    acc, m3 = weight_sums(an + an4 + b3, hid, 0, jnp.float32, m2)
    (d_own,) = pack(
        inner, [mid3, pair4, mid4, pair5],
        (((64, (0, 0), (1, 0)), (64, (2, 0), (3, 0))),),
        m3, c[1],
    )
    c3, c4 = fill(c3, c), fill(c4, [send(c[1], Y_ON)])
    d = ring(d_own)
    outs, m4 = hidden_grads(b4 + c3, offs, gate, up, wt, outs, m3)
    acc, m5 = weight_sums(b4 + c3, hid, 14 * HALF, jnp.float32, m4, acc=acc)
    d[1], = after([d[1]], m5)
    d3, d4 = fill(d3, d), fill(d4, [send(d[1], Y_ON)])
    outs, m6 = hidden_grads(d3, offs, gate, up, wt, outs, m5, params=WHOLE)
    early, lane = c4 + d3, 22 * HALF
    most, m7 = weight_sums(early, hid, lane, jnp.float32, m6, acc=acc, first=theirs, params=WHOLE)
    last_lane = lane + sum(r.shape[0] for r, _ in early)
    give, m7 = weight_sums(d4, hid, last_lane, jnp.bfloat16, m7, acc=most, first=theirs, params=WHOLE)
    got = send(give, DP_SWAP)
    outs, m8 = hidden_grads(c4 + d4, offs, gate, up, wt, outs, m7, params=WHOLE)
    factor = 1.0 / (2 * 64 * 8 * 16) ** 0.5
    weight_grad, _ = weight_sums(
        early + d4, hid, lane, jnp.bfloat16, m8, acc=acc, got=got, first=mine, factor=factor, params=WHOLE
    )
    return (outs[0][None, None], outs[1][None, None], weight_grad[None])


def solution(mesh):
    in_specs = (
        P("dp", ("expert", "tensor"), None),
        P("dp", ("expert", "tensor")),
        P("dp", ("expert", "tensor"), None),
        P("dp", "expert", None, "tensor"),
        P("dp", "expert", None, "tensor"),
        P("expert", "tensor", None),
    )
    out_specs = (
        P("dp", "expert", None, "tensor"),
        P("dp", "expert", None, "tensor"),
        P("expert", "tensor", "dp"),
    )
    return jax.shard_map(
        per_device, mesh=mesh, in_specs=in_specs, out_specs=out_specs, check_vma=False
    )
```
